256 devices in a mesh: win: 4 (over z_lo), row: 8 (over z_hi, x), col: 8 (over y, core).
Axes of the slice: x: 4, y: 4, z: 8 (z_hi: 2, z_lo: 4; z = z_hi * 4 + z_lo), core: 2. Of those that a mesh axis runs over, the one named last changes fastest.
Arguments:
- record: bfloat16 [32, 512, 12000], P('win', ('row', 'col')), may hold values from -6 to 6
- window_weight: float32 [32], P('win'), may hold values from 0.25 to 4
Outputs:
- corr: bfloat16 [8, 4, 16, 8, 64, 4000], P('row', 'win', None, None, 'col')
The draws below stay inside these ranges and needn't reach their ends.
All inputs are finite; a program needn't handle non-finite values.
Results may differ from the reference program's by a relative error of at most 0.0081.
Values may be sent and summed in bfloat16 or wider, within the bound.
No kernel may reach another device: no remote copies, remote signals or barrier semaphores. Data moves between devices by JAX's collectives and lax.ppermute only.
A program may use at most 192 MiB of HBM per device.

```python
import math
import jax
import jax.numpy as jnp
from jax import lax

SAMPLES = 12000
BINS = 512
LAGS = 4000
FIRST_BIN = 60
SMOOTH = 64
C = 512
NW = 32
N_WIN = 4
N_ROW = 8


def steps_of(own_key, dims, pieces, smallest, top_value):
    level = 1.0
    for axis_at, shards_of in pieces:
        heights = jax.random.uniform(jax.random.fold_in(jax.random.fold_in(own_key, 6), axis_at), (shards_of,), jnp.float32, smallest / len(pieces), top_value / len(pieces))
        level = level * jnp.repeat(jnp.exp(heights), dims[axis_at] // shards_of).reshape((-1,) + (1,) * (len(dims) - 1 - axis_at))
    return level


def bell_draw(own_key, dims, width, bound, split=(), kind=jnp.bfloat16):
    drawn = jax.random.normal(own_key, dims, jnp.float32) * width
    if len(split) > 0:
        drawn = steps_of(own_key, dims, split, -0.22, 0.18) * drawn
    return jnp.clip(drawn, min=-bound, max=bound).astype(kind)


def setup_inputs(seed: int = 0) -> dict:
    seeds = jax.random.split(jax.random.key(seed), 3)
    return {
        "record": bell_draw(seeds[0], (NW, C, SAMPLES), 1.0, 6.0, ((0, 4), (1, 64))),
        "window_weight": jnp.clip(jnp.exp(math.log(4.0) - 2.7725887 * jax.random.uniform(seeds[1], (NW,), jnp.float32) ** steps_of(seeds[1], (NW,), ((0, 4),), -0.2, 0.2)), 0.25, 4.0),
    }


def time_taper(length):
    index = jnp.arange(length, dtype=jnp.int32)
    edge = jnp.minimum(index, length - 1 - index).astype(jnp.float32)
    ramp = max(length // 20, 1)
    return jnp.where(edge < ramp, 0.5 - 0.5 * jnp.cos(jnp.pi * (edge + 0.5) / ramp), 1.0).astype(jnp.float32)

def band_taper(bins):
    index = jnp.arange(bins, dtype=jnp.int32)
    edge = jnp.minimum(index, bins - 1 - index).astype(jnp.float32)
    ramp = max(bins // 16, 1)
    return jnp.where(edge < ramp, 0.5 - 0.5 * jnp.cos(jnp.pi * (edge + 1.0) / (ramp + 1.0)), 1.0).astype(jnp.float32)

def fourier_table(length, bins, first):
    times = jnp.arange(length, dtype=jnp.int32)
    freqs = jnp.arange(bins, dtype=jnp.int32) + first
    phase = jnp.mod(times[:, None] * freqs[None, :], length).astype(jnp.float32)
    angle = 2.0 * jnp.pi / length * phase
    return jnp.concatenate([jnp.cos(angle), -jnp.sin(angle)], axis=1).astype(jnp.bfloat16)

def lag_table(length, bins, first, lags):
    shifts = jnp.arange(lags, dtype=jnp.int32) - lags // 2
    freqs = jnp.arange(bins, dtype=jnp.int32) + first
    phase = jnp.mod(freqs[:, None] * shifts[None, :], length).astype(jnp.float32)
    angle = 2.0 * jnp.pi / length * phase
    return jnp.concatenate([jnp.cos(angle), -jnp.sin(angle)], axis=0).astype(jnp.bfloat16)

def smoother(bins, half):
    index = jnp.arange(bins, dtype=jnp.int32)
    inside = (jnp.abs(index[:, None] - index[None, :]) <= half).astype(jnp.float32)
    return inside / lax.optimization_barrier(jnp.sum(inside, axis=0, keepdims=True))

def whiten(record, weights):
    windows, channels, length = record.shape
    values = record.astype(jnp.float32)
    centered = ((values - lax.optimization_barrier(jnp.mean(values, axis=2, keepdims=True))) * time_taper(length)).astype(jnp.bfloat16)
    table = fourier_table(length, BINS, FIRST_BIN)
    spectrum = jnp.dot(centered.reshape(-1, length), table, preferred_element_type=jnp.float32) * (1.0 / math.sqrt(length))
    real_part = spectrum[:, :BINS]
    imag_part = spectrum[:, BINS:]
    power = real_part * real_part + imag_part * imag_part
    smoothed = jnp.dot(power, smoother(BINS, SMOOTH), precision=lax.Precision.HIGHEST, preferred_element_type=jnp.float32)
    gain = band_taper(BINS)[None, :] / jnp.sqrt(smoothed + 1e-05)
    whitened = (spectrum * jnp.concatenate([gain, gain], axis=1)).reshape(windows, channels, 2 * BINS)
    plain = whitened.astype(jnp.bfloat16)
    weighted = (whitened * weights.astype(jnp.float32)[:, None, None]).astype(jnp.bfloat16)
    return (plain, weighted)

def cross(rows, cols):
    row_re = rows[..., :BINS].astype(jnp.float32)
    row_im = rows[..., BINS:].astype(jnp.float32)
    col_re = cols[..., :BINS].astype(jnp.float32)
    col_im = cols[..., BINS:].astype(jnp.float32)
    real_part = jnp.einsum('wif,wjf->ijf', row_re, col_re) + jnp.einsum('wif,wjf->ijf', row_im, col_im)
    imag_part = jnp.einsum('wif,wjf->ijf', row_im, col_re) - jnp.einsum('wif,wjf->ijf', row_re, col_im)
    return jnp.concatenate([real_part, imag_part], axis=2)

def reference(record, window_weight):
    windows, channels, length = record.shape
    plain, weighted = whiten(record, window_weight)
    table = lag_table(length, BINS, FIRST_BIN, LAGS)
    scale = 1.0 / math.sqrt(BINS * windows)
    block = math.gcd(channels, 32)
    starts = jnp.arange(channels // block, dtype=jnp.int32) * block

    def one_block(start):
        rows = lax.dynamic_slice_in_dim(weighted, start, block, 1)
        stacked = cross(rows, plain).astype(jnp.bfloat16)
        lagged = jnp.dot(stacked.reshape(-1, 2 * BINS), table, preferred_element_type=jnp.float32) * scale
        return lagged.astype(jnp.bfloat16).reshape(block, channels, LAGS)
    full = lax.map(one_block, starts).reshape(channels, channels, LAGS)
    row_block = channels // N_ROW
    return full.reshape(N_ROW, N_WIN, row_block // N_WIN, N_ROW, channels // N_ROW, LAGS)
```

```python
import math

import jax
import jax.numpy as jnp
import ml_dtypes
import numpy as np
from jax import lax
from jax.experimental import pallas as pl
from jax.experimental.pallas import tpu as pltpu
from jax.sharding import PartitionSpec as P

SAMPLES = 12000
QUARTER = 3000
BINS = 512
LAGS = 4000
LAGS_PAD = 4096
FIRST_BIN = 60
SMOOTH = 64
AXES = ("win", "row", "col")
OFFSETS = (0, -1, 1, -2, 2, -3, 3, -4)
BINS_AT = np.concatenate([np.arange(0, 512, 4), np.arange(2, 512, 4), np.arange(1, 512, 2)])
PHASE = 2.0 * np.pi / SAMPLES


def bf16(values):
    return values.astype(np.float32).astype(ml_dtypes.bfloat16)


def time_taper():
    index = np.arange(SAMPLES)
    edge = np.minimum(index, SAMPLES - 1 - index).astype(np.float64)
    ramp = max(SAMPLES // 20, 1)
    return np.where(edge < ramp, 0.5 - 0.5 * np.cos(np.pi * (edge + 0.5) / ramp), 1.0).astype(
        np.float32
    )


def band_taper():
    index = np.arange(BINS)
    edge = np.minimum(index, BINS - 1 - index).astype(np.float64)
    ramp = max(BINS // 16, 1)
    return np.where(edge < ramp, 0.5 - 0.5 * np.cos(np.pi * (edge + 1.0) / (ramp + 1.0)), 1.0).astype(
        np.float32
    )


def waves(bins):
    angle = PHASE * np.mod(np.arange(QUARTER)[:, None] * (bins + FIRST_BIN)[None, :], SAMPLES)
    return np.cos(angle), np.sin(angle)


def even_table(bins):
    cos, sin = waves(bins)
    return bf16(np.concatenate([cos, -sin], axis=1))


def odd_table(bins):
    cos, sin = waves(bins)
    turn = np.where((bins + FIRST_BIN) % 4 == 1, 1.0, -1.0)[None, :]
    first = np.concatenate([cos, -sin], axis=1)
    second = np.concatenate([-turn * sin, -turn * cos], axis=1)
    return bf16(np.concatenate([first, second], axis=0))


def lag_table():
    shifts = np.arange(LAGS) - LAGS // 2
    angle = PHASE * np.mod((BINS_AT + FIRST_BIN)[:, None] * shifts[None, :], SAMPLES)
    table = np.zeros((2 * BINS, LAGS_PAD))
    table[:BINS, :LAGS] = np.cos(angle)
    table[BINS:, :LAGS] = -np.sin(angle)
    return bf16(table)


def smoother():
    index = np.arange(BINS)
    inside = (np.abs(index[:, None] - index[None, :]) <= SMOOTH).astype(np.float32)
    mean = inside / np.sum(inside, axis=0, keepdims=True, dtype=np.float32)
    return mean[BINS_AT][:, BINS_AT]


def whiten(record, weights):
    windows, channels, length = record.shape
    values = record.reshape(windows * channels, length).astype(jnp.float32)
    centered = (values - jnp.mean(values, axis=1, keepdims=True)) * time_taper()[None, :]
    centered = centered.astype(jnp.bfloat16).astype(jnp.float32)
    part = [centered[:, QUARTER * q : QUARTER * (q + 1)] for q in range(4)]
    sum02, dif02 = part[0] + part[2], part[0] - part[2]
    sum13, dif13 = part[1] + part[3], part[1] - part[3]
    even0 = (sum02 + sum13).astype(jnp.bfloat16)
    even2 = (sum02 - sum13).astype(jnp.bfloat16)
    odd = jnp.concatenate([dif02, dif13], axis=1).astype(jnp.bfloat16)

    def product(left, table):
        return jnp.dot(left, table, preferred_element_type=jnp.float32)

    spec0 = product(even0, even_table(BINS_AT[:128]))
    spec2 = product(even2, even_table(BINS_AT[128:256]))
    spec1 = product(odd, odd_table(BINS_AT[256:]))
    scale = 1.0 / math.sqrt(length)
    real_part = jnp.concatenate([spec0[:, :128], spec2[:, :128], spec1[:, :256]], axis=1) * scale
    imag_part = jnp.concatenate([spec0[:, 128:], spec2[:, 128:], spec1[:, 256:]], axis=1) * scale
    power = real_part * real_part + imag_part * imag_part
    smoothed = jnp.dot(
        power,
        smoother(),
        precision=lax.Precision.HIGHEST,
        preferred_element_type=jnp.float32,
    )
    gain = band_taper()[BINS_AT][None, :] / jnp.sqrt(smoothed + 1e-05)
    whitened = jnp.concatenate([real_part * gain, imag_part * gain], axis=1)
    whitened = whitened.reshape(windows, channels, 2 * BINS)
    plain = whitened.astype(jnp.bfloat16)
    weighted = (whitened * weights[:, None, None]).astype(jnp.bfloat16)
    return plain, weighted


def device_at(x, y, z, core):
    return ((z % 4) * 8 + (z // 4) * 4 + x) * 8 + y * 2 + core


def shift(value, dx=0, dy=0, dz=0, dcore=0):
    pairs = [
        (
            device_at(x, y, z, core),
            device_at((x + dx) % 4, (y + dy) % 4, (z + dz) % 8, (core + dcore) % 2),
        )
        for x in range(4)
        for y in range(4)
        for z in range(8)
        for core in range(2)
    ]
    return lax.ppermute(value, AXES, pairs)


def ring_z(own):
    blocks = [own]
    up = down = own
    for step in range(1, 5):
        up = shift(up, dz=1)
        blocks.append(up)
        if step < 4:
            down = shift(down, dz=-1)
            blocks.append(down)
    return blocks


def spread_x(own):
    return [own, shift(own, dx=1), shift(own, dx=-1), shift(own, dx=2)]


def gather_cols(plain):
    half = plain.shape[0] // 2
    first = spread_x(jnp.stack(ring_z(plain[:half])))
    second = ring_z(jnp.stack(spread_x(plain[half:])))
    return jnp.stack(first), jnp.stack(second)


def gather_rows(weighted, y, z_low):
    held = jnp.stack([weighted] + [shift(weighted, dy=k) for k in (1, 2, 3)])

    def for_offset(k):
        return lax.dynamic_index_in_dim(held, (y - z_low - k) % 4, 0, keepdims=False)

    moved = [for_offset(0)]
    for k in (1, 2, 3):
        moved.append(lax.ppermute(for_offset(k), "win", [(i, (i + k) % 4) for i in range(4)]))
    mine = jnp.stack(moved)
    return mine, shift(mine, dcore=1)


def pair_kernel(place, first, second, mine, other, table, out, z_re, z_im, z_sum, stack):
    chunk = pl.program_id(0)

    @pl.when(chunk == 0)
    def _():
        core = place[16]
        for k in range(4):
            group = place[12 + k]
            for ref, at in ((mine, core), (other, 1 - core)):
                for w in range(8):
                    value = ref[k, w].astype(jnp.float32)
                    re, im = value[:, :BINS], value[:, BINS:]
                    z_re[group * 8 + w, at] = re
                    z_im[group * 8 + w, at] = im
                    z_sum[group * 8 + w, at] = re + im

    def cross_block(lane, block):
        lane_im = pl.multiple_of(lane + BINS, 128)
        core, base = block // 2, (block % 2) * 4

        def group_step(group, sums):
            sums = list(sums)
            at = [place[4 + group], place[8 + group]]
            for w in range(8):
                source, v = (first, w) if w < 4 else (second, w - 4)
                yr, yi = [], []
                for high in range(2):
                    where = (0, at[high], v) if w < 4 else (at[high], 0, v)
                    yr.append(source[(*where, slice(None), pl.ds(lane, 128))].astype(jnp.float32))
                    yi.append(source[(*where, slice(None), pl.ds(lane_im, 128))].astype(jnp.float32))
                dif = [yr[0] - yi[0], yr[1] - yi[1]]
                window = group * 8 + w
                for i in range(4):
                    row = pl.ds(base + i, 1)
                    zr = jnp.broadcast_to(z_re[window, core, row, pl.ds(lane, 128)], (8, 128))
                    zi = jnp.broadcast_to(z_im[window, core, row, pl.ds(lane, 128)], (8, 128))
                    zs = jnp.broadcast_to(z_sum[window, core, row, pl.ds(lane, 128)], (8, 128))
                    for high in range(2):
                        n = (i * 2 + high) * 3
                        sums[n] = sums[n] + zr * yr[high]
                        sums[n + 1] = sums[n + 1] + zi * yi[high]
                        sums[n + 2] = sums[n + 2] + zs * dif[high]
            return tuple(sums)

        sums = lax.fori_loop(0, 4, group_step, (jnp.zeros((8, 128), jnp.float32),) * 24)
        for i in range(4):
            re, im = [], []
            for high in range(2):
                p, q, r = sums[(i * 2 + high) * 3 : (i * 2 + high) * 3 + 3]
                re.append(p + q)
                im.append(r - p + q)
            row = pl.ds((block * 4 + i) * 16, 16)
            stack[row, pl.ds(lane, 128)] = jnp.concatenate(re, axis=0).astype(jnp.bfloat16)
            stack[row, pl.ds(lane_im, 128)] = jnp.concatenate(im, axis=0).astype(jnp.bfloat16)

    def cross(tile, carry):
        lane = pl.multiple_of(tile * 128, 128)
        for block in range(4):
            cross_block(lane, block)
        return carry

    lax.fori_loop(0, 4, cross, 0)
    width = 512
    for tile in range(LAGS_PAD // width):
        start = tile * width
        keep = min(width, LAGS - start)
        value = jnp.dot(
            stack[...], table[:, start : start + width], preferred_element_type=jnp.float32
        )
        value = value * (1.0 / 128.0)
        value = value.reshape(16, 2, 1, 8, width).astype(jnp.bfloat16)
        out[:, :, :, :, start : start + keep] = value[..., :keep]


def pair_correlations(place, first, second, mine, other):
    whole = pl.BlockSpec(memory_space=pltpu.VMEM)
    return pl.pallas_call(
        pair_kernel,
        out_shape=jax.ShapeDtypeStruct((16, 2, 4, 8, LAGS), jnp.bfloat16),
        grid_spec=pltpu.PrefetchScalarGridSpec(
            num_scalar_prefetch=1,
            grid=(4,),
            in_specs=[
                pl.BlockSpec((1, 8, 4, 8, 2 * BINS), lambda j, place: (j, 0, 0, 0, 0)),
                pl.BlockSpec((8, 1, 4, 8, 2 * BINS), lambda j, place: (0, j, 0, 0, 0)),
                whole,
                whole,
                whole,
            ],
            out_specs=pl.BlockSpec((16, 2, 1, 8, LAGS), lambda j, place: (0, 0, place[j], 0, 0)),
            scratch_shapes=[
                pltpu.VMEM((32, 2, 8, BINS), jnp.float32),
                pltpu.VMEM((32, 2, 8, BINS), jnp.float32),
                pltpu.VMEM((32, 2, 8, BINS), jnp.float32),
                pltpu.VMEM((256, 2 * BINS), jnp.bfloat16),
            ],
        ),
        compiler_params=pltpu.CompilerParams(vmem_limit_bytes=48 * 1024 * 1024),
        cost_estimate=pl.CostEstimate(
            flops=2 * 1024 * 1024 * LAGS, bytes_accessed=24 * 2**20, transcendentals=0
        ),
    )(place, first, second, mine, other, lag_table())


def shards(record, window_weight):
    plain, weighted = whiten(record, window_weight)
    z_low = lax.axis_index("win")
    row = lax.axis_index("row")
    col = lax.axis_index("col")
    z_high, x = row // 4, row % 4
    z = z_high * 4 + z_low
    mine, other = gather_rows(weighted, col // 2, z_low)
    first, second = gather_cols(plain)
    slots = np.zeros(8, np.int32)
    for slot, offset in enumerate(OFFSETS):
        slots[offset % 8] = slot
    slot_of = jnp.asarray(slots)[(jnp.arange(8) - z) % 8]
    place = jnp.concatenate(
        [
            (x + jnp.array([0, -1, 1, 2])) % 4,
            slot_of,
            (z_low - jnp.arange(4)) % 4,
            jnp.stack([col % 2]),
        ]
    ).astype(jnp.int32)
    corr = pair_correlations(place, first, second, mine, other)
    return corr.reshape(1, 1, 16, 8, 8, LAGS)


def solution(mesh):
    placed = (P("win", ("row", "col"), None), P("win"))
    return jax.shard_map(
        shards,
        mesh=mesh,
        in_specs=placed,
        out_specs=P("row", "win", None, None, "col", None),
        check_vma=False,
    )
```

```python
import math

import jax
import jax.numpy as jnp
import ml_dtypes
import numpy as np
from jax import lax
from jax.experimental import pallas as pl
from jax.experimental.pallas import tpu as pltpu
from jax.sharding import PartitionSpec as P

SAMPLES = 12000
QUARTER = 3000
BINS = 512
LAGS = 4000
LAGS_PAD = 4096
FIRST_BIN = 60
SMOOTH = 64
AXES = ("win", "row", "col")
BINS_AT = np.concatenate([np.arange(0, 512, 4), np.arange(2, 512, 4), np.arange(1, 512, 2)])
PHASE = 2.0 * np.pi / SAMPLES


def bf16(values):
    return values.astype(np.float32).astype(ml_dtypes.bfloat16)


def time_taper():
    index = np.arange(SAMPLES)
    edge = np.minimum(index, SAMPLES - 1 - index).astype(np.float64)
    ramp = max(SAMPLES // 20, 1)
    return np.where(edge < ramp, 0.5 - 0.5 * np.cos(np.pi * (edge + 0.5) / ramp), 1.0).astype(
        np.float32
    )


def band_taper():
    index = np.arange(BINS)
    edge = np.minimum(index, BINS - 1 - index).astype(np.float64)
    ramp = max(BINS // 16, 1)
    return np.where(edge < ramp, 0.5 - 0.5 * np.cos(np.pi * (edge + 1.0) / (ramp + 1.0)), 1.0).astype(
        np.float32
    )


def waves(bins):
    angle = PHASE * np.mod(np.arange(QUARTER)[:, None] * (bins + FIRST_BIN)[None, :], SAMPLES)
    return np.cos(angle), np.sin(angle)


def even_table(bins):
    cos, sin = waves(bins)
    return bf16(np.concatenate([cos, -sin], axis=1))


def odd_table(bins):
    cos, sin = waves(bins)
    turn = np.where((bins + FIRST_BIN) % 4 == 1, 1.0, -1.0)[None, :]
    first = np.concatenate([cos, -sin], axis=1)
    second = np.concatenate([-turn * sin, -turn * cos], axis=1)
    return bf16(np.concatenate([first, second], axis=0))


def lag_table():
    shifts = np.arange(LAGS) - LAGS // 2
    angle = PHASE * np.mod((BINS_AT + FIRST_BIN)[:, None] * shifts[None, :], SAMPLES)
    table = np.zeros((2 * BINS, LAGS_PAD))
    table[:BINS, :LAGS] = np.cos(angle)
    table[BINS:, :LAGS] = -np.sin(angle)
    return bf16(table / 128.0)


def smoother():
    index = np.arange(BINS)
    inside = (np.abs(index[:, None] - index[None, :]) <= SMOOTH).astype(np.float32)
    mean = inside / np.sum(inside, axis=0, keepdims=True, dtype=np.float32)
    return mean[BINS_AT][:, BINS_AT]


def whiten(record, weights):
    windows, channels, length = record.shape
    values = record.reshape(windows * channels, length).astype(jnp.float32)
    centered = (values - jnp.mean(values, axis=1, keepdims=True)) * time_taper()[None, :]
    centered = centered.astype(jnp.bfloat16).astype(jnp.float32)
    part = [centered[:, QUARTER * q : QUARTER * (q + 1)] for q in range(4)]
    sum02, dif02 = part[0] + part[2], part[0] - part[2]
    sum13, dif13 = part[1] + part[3], part[1] - part[3]
    even0 = (sum02 + sum13).astype(jnp.bfloat16)
    even2 = (sum02 - sum13).astype(jnp.bfloat16)
    odd = jnp.concatenate([dif02, dif13], axis=1).astype(jnp.bfloat16)

    def product(left, table):
        return jnp.dot(left, table, preferred_element_type=jnp.float32)

    spec0 = product(even0, even_table(BINS_AT[:128]))
    spec2 = product(even2, even_table(BINS_AT[128:256]))
    spec1 = product(odd, odd_table(BINS_AT[256:]))
    scale = 1.0 / math.sqrt(length)
    real_part = jnp.concatenate([spec0[:, :128], spec2[:, :128], spec1[:, :256]], axis=1) * scale
    imag_part = jnp.concatenate([spec0[:, 128:], spec2[:, 128:], spec1[:, 256:]], axis=1) * scale
    power = real_part * real_part + imag_part * imag_part
    smoothed = jnp.dot(
        power,
        smoother(),
        precision=lax.Precision.HIGHEST,
        preferred_element_type=jnp.float32,
    )
    gain = band_taper()[BINS_AT][None, :] / jnp.sqrt(smoothed + 1e-05)
    whitened = jnp.concatenate([real_part * gain, imag_part * gain], axis=1)
    whitened = whitened.reshape(windows, channels, 2 * BINS)
    plain = whitened.astype(jnp.bfloat16)
    weighted = (whitened * weights[:, None, None]).astype(jnp.bfloat16)
    return plain, weighted


def device_at(x, y, z, core):
    return ((z % 4) * 8 + (z // 4) * 4 + x) * 8 + y * 2 + core


def shift(value, dx=0, dy=0, dz=0, dcore=0):
    pairs = [
        (
            device_at(x, y, z, core),
            device_at((x + dx) % 4, (y + dy) % 4, (z + dz) % 8, (core + dcore) % 2),
        )
        for x in range(4)
        for y in range(4)
        for z in range(8)
        for core in range(2)
    ]
    return lax.ppermute(value, AXES, pairs)


def own_only(value, k):
    return lax.ppermute(value, "win", [(i, (i + k) % 4) for i in range(4)])


def together(*values):
    return lax.optimization_barrier(values)


def first_step(plain, weighted):
    return together(
        shift(plain, dz=4),
        shift(plain, dx=2),
        shift(plain, dz=1),
        shift(plain, dz=-1),
        shift(weighted, dy=1),
        shift(weighted, dy=2),
        shift(weighted, dy=3),
    )


def second_step(plain, weighted, arrived, y, z_low):
    opposite, across, below, above, *sides = arrived
    near = jnp.stack([plain, below, above, opposite])
    held = jnp.stack([weighted, *sides])

    def for_offset(k):
        return lax.dynamic_index_in_dim(held, (y - z_low - k) % 4, 0, keepdims=False)

    sent = together(
        shift(near, dx=1),
        shift(near, dx=-1),
        shift(jnp.stack([below, opposite, across]), dz=1),
        shift(jnp.stack([above, opposite, across]), dz=-1),
        shift(opposite, dx=2),
        own_only(for_offset(1), 1),
        own_only(for_offset(2), 2),
        own_only(for_offset(3), 3),
    )
    left, right, up, down, across_opposite, *rows = sent
    far = jnp.concatenate([up[:2], down[:2]])
    across_near = jnp.stack([across, up[2], down[2], across_opposite])
    mine = jnp.stack([for_offset(0), *rows])
    return near, far, left, right, across_near, mine


def third_step(far, across_near):
    left, right, up, down = together(
        shift(far, dx=1),
        shift(far, dx=-1),
        shift(across_near[1::2], dz=1),
        shift(across_near[2:], dz=-1),
    )
    return jnp.stack([left, right, jnp.concatenate([up, down])])


NEAR = (0, -1, 1, 4)
FAR = (-2, 3, 2, -3)
XS, HIGH_NEAR, GROUP_NEAR, HIGH_FAR, GROUP_FAR, ROWS, CORE = 0, 4, 8, 12, 16, 20, 24


def load_rows(place, mine, other, z_re, z_im, z_sum):
    core = place[CORE]
    for k in range(4):
        group = place[ROWS + k]
        for ref, at in ((mine, core), (other, 1 - core)):
            for w in range(8):
                value = ref[k, w].astype(jnp.float32)
                re, im = value[:, :BINS], value[:, BINS:]
                for tile in range(4):
                    lanes = slice(tile * 128, tile * 128 + 128)
                    z_re[group * 8 + w, at, tile] = re[:, lanes]
                    z_im[group * 8 + w, at, tile] = im[:, lanes]
                    z_sum[group * 8 + w, at, tile] = re[:, lanes] + im[:, lanes]


def add_cross(turn, block, high_at, group_at, place, z_re, z_im, z_sum, total):
    tile, n = turn // 4, turn % 4
    lane = pl.ds(pl.multiple_of(tile * 128, 128), 128)
    lane_im = pl.ds(pl.multiple_of(tile * 128 + BINS, 128), 128)
    high, group = place[high_at + n], place[group_at + n]
    for core, base in ((0, 0), (0, 4), (1, 0), (1, 4)):
        sums = [None] * 12
        for w in range(8):
            yr = block[0, n, w, :, lane].astype(jnp.float32)
            yi = block[0, n, w, :, lane_im].astype(jnp.float32)
            dif = yr - yi
            window = group * 8 + w
            for i in range(4):
                row = pl.ds(base + i, 8, stride=0)
                terms = (
                    z_re[window, core, tile, row, :] * yr,
                    z_im[window, core, tile, row, :] * yi,
                    z_sum[window, core, tile, row, :] * dif,
                )
                for m, term in enumerate(terms):
                    at = i * 3 + m
                    sums[at] = term if w == 0 else sums[at] + term
        for i in range(4):
            p, q, r = sums[i * 3 : i * 3 + 3]
            total[high, core * 8 + base + i, :, lane] += p + q
            total[high, core * 8 + base + i, :, lane_im] += r - p + q


def near_kernel(place, block, mine, other, total, z_re, z_im, z_sum):
    step = pl.program_id(0)

    @pl.when(step == 0)
    def _():
        load_rows(place, mine, other, z_re, z_im, z_sum)

    @pl.when(step != 1)
    def _():
        total[...] = jnp.zeros_like(total)

    high_at = jnp.where(step == 1, HIGH_FAR, HIGH_NEAR)
    group_at = jnp.where(step == 1, GROUP_FAR, GROUP_NEAR)

    def turn(at, carry):
        add_cross(at, block, high_at, group_at, place, z_re, z_im, z_sum, total.at[0])
        return carry

    lax.fori_loop(0, 16, turn, 0)


WHOLE = pl.BlockSpec(memory_space=pltpu.VMEM)
BLOCK = (1, 4, 8, 8, 2 * BINS)
TOTAL = (1, 2, 16, 8, 2 * BINS)
ROW_SCRATCH = [pltpu.VMEM((32, 2, 4, 8, 128), jnp.float32)] * 3


def near_totals(place, blocks, mine, other):
    return pl.pallas_call(
        near_kernel,
        out_shape=jax.ShapeDtypeStruct((4, *TOTAL[1:]), jnp.float32),
        grid_spec=pltpu.PrefetchScalarGridSpec(
            num_scalar_prefetch=1,
            grid=(5,),
            in_specs=[
                pl.BlockSpec(BLOCK, lambda j, place: (j, 0, 0, 0, 0)),
                WHOLE,
                WHOLE,
            ],
            out_specs=pl.BlockSpec(TOTAL, lambda j, place: (jnp.maximum(j - 1, 0), 0, 0, 0, 0)),
            scratch_shapes=ROW_SCRATCH,
        ),
        compiler_params=pltpu.CompilerParams(vmem_limit_bytes=32 * 1024 * 1024),
        cost_estimate=pl.CostEstimate(
            flops=12 * 10**9, bytes_accessed=8 * 2**20, transcendentals=0
        ),
    )(place, blocks, mine, other)


def far_kernel(
    place, block, before, mine, other, source, out, z_re, z_im, z_sum, total, now, later, table, ready
):
    step = pl.program_id(0)
    fetch = pltpu.make_async_copy(source, table, ready)

    def settle(source, target):
        for i in range(16):
            rows = jnp.concatenate([source[0, i], source[1, i]], axis=0)
            target[pl.ds(i * 16, 16), :] = rows.astype(jnp.bfloat16)

    @pl.when(step == 0)
    def _():
        fetch.start()
        load_rows(place, mine, other, z_re, z_im, z_sum)
        settle(before.at[0], now)

    def lag_all():
        for tile in range(8):
            start = tile * 512
            keep = min(512, LAGS - start)
            value = jnp.dot(
                now[...], table[:, start : start + 512], preferred_element_type=jnp.float32
            )
            value = value.reshape(16, 2, 1, 8, 512).astype(jnp.bfloat16)
            out[:, :, :, :, start : start + keep] = value[..., :keep]

    @pl.when(step < 3)
    def _():
        total[...] = before[step + 1]

        def turn(at, carry):
            add_cross(at, block, HIGH_FAR, GROUP_FAR, place, z_re, z_im, z_sum, total)
            return carry

        lax.fori_loop(0, 16, turn, 0)
        settle(total, later)

    @pl.when(step == 0)
    def _():
        fetch.wait()

    lag_all()

    @pl.when(step < 3)
    def _():
        now[...] = later[...]


def correlations(place, blocks, before, mine, other):
    last = lambda j: jnp.minimum(j, 2)
    return pl.pallas_call(
        far_kernel,
        out_shape=jax.ShapeDtypeStruct((16, 2, 4, 8, LAGS), jnp.bfloat16),
        grid_spec=pltpu.PrefetchScalarGridSpec(
            num_scalar_prefetch=1,
            grid=(4,),
            in_specs=[
                pl.BlockSpec(BLOCK, lambda j, place: (last(j), 0, 0, 0, 0)),
                pl.BlockSpec((4, *TOTAL[1:]), lambda j, place: (0, 0, 0, 0, 0)),
                WHOLE,
                WHOLE,
                pl.BlockSpec(memory_space=pl.ANY),
            ],
            out_specs=pl.BlockSpec((16, 2, 1, 8, LAGS), lambda j, place: (0, 0, place[j], 0, 0)),
            scratch_shapes=[
                *ROW_SCRATCH,
                pltpu.VMEM(TOTAL[1:], jnp.float32),
                pltpu.VMEM((256, 2 * BINS), jnp.bfloat16),
                pltpu.VMEM((256, 2 * BINS), jnp.bfloat16),
                pltpu.VMEM((2 * BINS, LAGS_PAD), jnp.bfloat16),
                pltpu.SemaphoreType.DMA(()),
            ],
        ),
        compiler_params=pltpu.CompilerParams(vmem_limit_bytes=48 * 1024 * 1024),
        cost_estimate=pl.CostEstimate(
            flops=2 * 1024 * 1024 * LAGS, bytes_accessed=24 * 2**20, transcendentals=0
        ),
    )(place, blocks, before, mine, other, lag_table())


def shards(record, window_weight):
    plain, weighted = whiten(record, window_weight)
    z_low = lax.axis_index("win")
    row = lax.axis_index("row")
    col = lax.axis_index("col")
    x, z = row % 4, (row // 4) * 4 + z_low
    near_z = (z + jnp.array(NEAR)) % 8
    far_z = (z + jnp.array(FAR)) % 8
    place = jnp.concatenate(
        [
            (x + jnp.array([0, -1, 1, 2])) % 4,
            near_z // 4,
            near_z % 4,
            far_z // 4,
            far_z % 4,
            (z_low - jnp.arange(4)) % 4,
            jnp.stack([col % 2]),
        ]
    ).astype(jnp.int32)
    arrived = first_step(plain, weighted)
    near, far, left, right, across, mine = second_step(plain, weighted, arrived, col // 2, z_low)
    other = shift(mine, dcore=1)
    rest = third_step(far, across)
    before = near_totals(place, jnp.stack([near, far, left, right, across]), mine, other)
    corr = correlations(place, rest, before, mine, other)
    return corr.reshape(1, 1, 16, 8, 8, LAGS)


def solution(mesh):
    placed = (P("win", ("row", "col"), None), P("win"))
    return jax.shard_map(
        shards,
        mesh=mesh,
        in_specs=placed,
        out_specs=P("row", "win", None, None, "col", None),
        check_vma=False,
    )
```

```python
import math

import jax
import jax.numpy as jnp
import ml_dtypes
import numpy as np
from jax import lax
from jax.experimental import pallas as pl
from jax.experimental.pallas import tpu as pltpu
from jax.sharding import PartitionSpec as P

SAMPLES = 12000
QUARTER = 3000
BINS = 512
LAGS = 4000
LAGS_PAD = 4096
FIRST_BIN = 60
SMOOTH = 64
AXES = ("win", "row", "col")
BINS_AT = np.concatenate([np.arange(0, 512, 4), np.arange(2, 512, 4), np.arange(1, 512, 2)])
PHASE = 2.0 * np.pi / SAMPLES


def bf16(values):
    return values.astype(np.float32).astype(ml_dtypes.bfloat16)


def time_taper():
    index = np.arange(SAMPLES)
    edge = np.minimum(index, SAMPLES - 1 - index).astype(np.float64)
    ramp = max(SAMPLES // 20, 1)
    return np.where(edge < ramp, 0.5 - 0.5 * np.cos(np.pi * (edge + 0.5) / ramp), 1.0).astype(
        np.float32
    )


def band_taper():
    index = np.arange(BINS)
    edge = np.minimum(index, BINS - 1 - index).astype(np.float64)
    ramp = max(BINS // 16, 1)
    return np.where(edge < ramp, 0.5 - 0.5 * np.cos(np.pi * (edge + 1.0) / (ramp + 1.0)), 1.0).astype(
        np.float32
    )


def waves(bins):
    angle = PHASE * np.mod(np.arange(QUARTER)[:, None] * (bins + FIRST_BIN)[None, :], SAMPLES)
    return np.cos(angle), np.sin(angle)


def even_table(bins):
    cos, sin = waves(bins)
    return bf16(np.concatenate([cos, -sin], axis=1))


def odd_table(bins):
    cos, sin = waves(bins)
    turn = np.where((bins + FIRST_BIN) % 4 == 1, 1.0, -1.0)[None, :]
    first = np.concatenate([cos, -sin], axis=1)
    second = np.concatenate([-turn * sin, -turn * cos], axis=1)
    return bf16(np.concatenate([first, second], axis=0))


def lag_table():
    shifts = np.arange(LAGS) - LAGS // 2
    angle = PHASE * np.mod((BINS_AT + FIRST_BIN)[:, None] * shifts[None, :], SAMPLES)
    table = np.zeros((2 * BINS, LAGS_PAD))
    table[:BINS, :LAGS] = np.cos(angle)
    table[BINS:, :LAGS] = -np.sin(angle)
    return bf16(table / 128.0)


def smoother():
    index = np.arange(BINS)
    inside = (np.abs(index[:, None] - index[None, :]) <= SMOOTH).astype(np.float32)
    mean = inside / np.sum(inside, axis=0, keepdims=True, dtype=np.float32)
    return mean[BINS_AT][:, BINS_AT]


def whiten(record, weights):
    windows, channels, length = record.shape
    values = record.reshape(windows * channels, length).astype(jnp.float32)
    centered = (values - jnp.mean(values, axis=1, keepdims=True)) * time_taper()[None, :]
    centered = centered.astype(jnp.bfloat16).astype(jnp.float32)
    part = [centered[:, QUARTER * q : QUARTER * (q + 1)] for q in range(4)]
    sum02, dif02 = part[0] + part[2], part[0] - part[2]
    sum13, dif13 = part[1] + part[3], part[1] - part[3]
    even0 = (sum02 + sum13).astype(jnp.bfloat16)
    even2 = (sum02 - sum13).astype(jnp.bfloat16)
    odd = jnp.concatenate([dif02, dif13], axis=1).astype(jnp.bfloat16)

    def product(left, table):
        return jnp.dot(left, table, preferred_element_type=jnp.float32)

    spec0 = product(even0, even_table(BINS_AT[:128]))
    spec2 = product(even2, even_table(BINS_AT[128:256]))
    spec1 = product(odd, odd_table(BINS_AT[256:]))
    scale = 1.0 / math.sqrt(length)
    real_part = jnp.concatenate([spec0[:, :128], spec2[:, :128], spec1[:, :256]], axis=1) * scale
    imag_part = jnp.concatenate([spec0[:, 128:], spec2[:, 128:], spec1[:, 256:]], axis=1) * scale
    power = real_part * real_part + imag_part * imag_part
    smoothed = jnp.dot(
        power,
        smoother(),
        precision=lax.Precision.HIGHEST,
        preferred_element_type=jnp.float32,
    )
    gain = band_taper()[BINS_AT][None, :] / jnp.sqrt(smoothed + 1e-05)
    whitened = jnp.concatenate([real_part * gain, imag_part * gain], axis=1)
    whitened = whitened.reshape(windows, channels, 2 * BINS)
    plain = whitened.astype(jnp.bfloat16)
    weighted = (whitened * weights[:, None, None]).astype(jnp.bfloat16)
    return plain, weighted


def device_at(x, y, z, core):
    return ((z % 4) * 8 + (z // 4) * 4 + x) * 8 + y * 2 + core


def shift(value, dx=0, dy=0, dz=0, dcore=0):
    pairs = [
        (
            device_at(x, y, z, core),
            device_at((x + dx) % 4, (y + dy) % 4, (z + dz) % 8, (core + dcore) % 2),
        )
        for x in range(4)
        for y in range(4)
        for z in range(8)
        for core in range(2)
    ]
    return lax.ppermute(value, AXES, pairs)


def turn_rows(value, m):
    pairs = []
    for x in range(4):
        for high in range(2):
            for y in range(4):
                for low in range(4):
                    for core in range(2):
                        k = 2 * core + m
                        source = device_at(x, y, high * 4 + low, core)
                        pairs.append((source, device_at(x, (low - k) % 4, high * 4 + y, core)))
    return lax.ppermute(value, AXES, pairs)


def together(*values):
    return lax.optimization_barrier(values)


def first_step(plain, weighted):
    both = jnp.stack([weighted, shift(weighted, dcore=1)])
    return together(
        shift(plain, dz=4),
        shift(plain, dx=2),
        shift(plain, dz=1),
        shift(plain, dz=-1),
        turn_rows(both, 0),
        turn_rows(both, 1),
    )


def second_step(plain, arrived):
    opposite, across, below, above, *turned = arrived
    near = jnp.stack([plain, below, above, opposite])
    mine = jnp.stack(turned)
    other, left, right, up, down, across_opposite = together(
        shift(mine, dcore=1),
        shift(near, dx=1),
        shift(near, dx=-1),
        shift(jnp.stack([below, opposite, across]), dz=1),
        shift(jnp.stack([above, opposite, across]), dz=-1),
        shift(opposite, dx=2),
    )
    far = jnp.concatenate([up[:2], down[:2]])
    across_near = jnp.stack([across, up[2], down[2], across_opposite])
    return near, far, left, right, across_near, mine, other


def third_step(far, across_near):
    left, right, up, down = together(
        shift(far, dx=1),
        shift(far, dx=-1),
        shift(across_near[1::2], dz=1),
        shift(across_near[2:], dz=-1),
    )
    return jnp.stack([left, right, jnp.concatenate([up, down])])


NEAR = (0, -1, 1, 4)
FAR = (-2, 3, 2, -3)
XS, HIGH_NEAR, GROUP_NEAR, HIGH_FAR, GROUP_FAR, ROWS, CORE = 0, 4, 8, 12, 16, 20, 24


def load_rows(place, mine, other, z_re, z_im, z_sum):
    core = place[CORE]
    for k in range(4):
        ref, m = (mine, k) if k < 2 else (other, k - 2)
        group = place[ROWS + k]
        for n in range(2):
            at = core if (k < 2) == (n == 0) else 1 - core
            for w in range(8):
                value = ref[m, n, w].astype(jnp.float32)
                re, im = value[:, :BINS], value[:, BINS:]
                for tile in range(4):
                    lanes = slice(tile * 128, tile * 128 + 128)
                    z_re[group * 8 + w, at, tile] = re[:, lanes]
                    z_im[group * 8 + w, at, tile] = im[:, lanes]
                    z_sum[group * 8 + w, at, tile] = re[:, lanes] + im[:, lanes]


def add_cross(turn, block, high_at, group_at, place, z_re, z_im, z_sum, total):
    tile, n = turn // 4, turn % 4
    lane = pl.ds(pl.multiple_of(tile * 128, 128), 128)
    lane_im = pl.ds(pl.multiple_of(tile * 128 + BINS, 128), 128)
    high, group = place[high_at + n], place[group_at + n]
    for core, base in ((0, 0), (0, 4), (1, 0), (1, 4)):
        sums = [None] * 12
        for w in range(8):
            yr = block[0, n, w, :, lane].astype(jnp.float32)
            yi = block[0, n, w, :, lane_im].astype(jnp.float32)
            dif = yr - yi
            window = group * 8 + w
            for i in range(4):
                row = pl.ds(base + i, 8, stride=0)
                terms = (
                    z_re[window, core, tile, row, :] * yr,
                    z_im[window, core, tile, row, :] * yi,
                    z_sum[window, core, tile, row, :] * dif,
                )
                for m, term in enumerate(terms):
                    at = i * 3 + m
                    sums[at] = term if w == 0 else sums[at] + term
        for i in range(4):
            p, q, r = sums[i * 3 : i * 3 + 3]
            total[high, core * 8 + base + i, :, lane] += p + q
            total[high, core * 8 + base + i, :, lane_im] += r - p + q


def near_kernel(place, block, mine, other, total, z_re, z_im, z_sum):
    step = pl.program_id(0)

    @pl.when(step == 0)
    def _():
        load_rows(place, mine, other, z_re, z_im, z_sum)

    @pl.when(step != 1)
    def _():
        total[...] = jnp.zeros_like(total)

    high_at = jnp.where(step == 1, HIGH_FAR, HIGH_NEAR)
    group_at = jnp.where(step == 1, GROUP_FAR, GROUP_NEAR)

    def turn(at, carry):
        add_cross(at, block, high_at, group_at, place, z_re, z_im, z_sum, total.at[0])
        return carry

    lax.fori_loop(0, 16, turn, 0)


WHOLE = pl.BlockSpec(memory_space=pltpu.VMEM)
BLOCK = (1, 4, 8, 8, 2 * BINS)
TOTAL = (1, 2, 16, 8, 2 * BINS)
ROW_SCRATCH = [pltpu.VMEM((32, 2, 4, 8, 128), jnp.float32)] * 3


def near_totals(place, blocks, mine, other):
    return pl.pallas_call(
        near_kernel,
        out_shape=jax.ShapeDtypeStruct((4, *TOTAL[1:]), jnp.float32),
        grid_spec=pltpu.PrefetchScalarGridSpec(
            num_scalar_prefetch=1,
            grid=(5,),
            in_specs=[
                pl.BlockSpec(BLOCK, lambda j, place: (j, 0, 0, 0, 0)),
                WHOLE,
                WHOLE,
            ],
            out_specs=pl.BlockSpec(TOTAL, lambda j, place: (jnp.maximum(j - 1, 0), 0, 0, 0, 0)),
            scratch_shapes=ROW_SCRATCH,
        ),
        compiler_params=pltpu.CompilerParams(vmem_limit_bytes=32 * 1024 * 1024),
        cost_estimate=pl.CostEstimate(
            flops=12 * 10**9, bytes_accessed=8 * 2**20, transcendentals=0
        ),
    )(place, blocks, mine, other)


def far_kernel(
    place, block, before, mine, other, source, out, z_re, z_im, z_sum, total, now, later, table, ready
):
    step = pl.program_id(0)
    fetch = pltpu.make_async_copy(source, table, ready)

    def settle(source, target):
        for i in range(16):
            rows = jnp.concatenate([source[0, i], source[1, i]], axis=0)
            target[pl.ds(i * 16, 16), :] = rows.astype(jnp.bfloat16)

    @pl.when(step == 0)
    def _():
        fetch.start()
        load_rows(place, mine, other, z_re, z_im, z_sum)
        settle(before.at[0], now)

    def lag_all():
        for tile in range(8):
            start = tile * 512
            keep = min(512, LAGS - start)
            value = jnp.dot(
                now[...], table[:, start : start + 512], preferred_element_type=jnp.float32
            )
            value = value.reshape(16, 2, 1, 8, 512).astype(jnp.bfloat16)
            out[:, :, :, :, start : start + keep] = value[..., :keep]

    @pl.when(step < 3)
    def _():
        total[...] = before[step + 1]

        def turn(at, carry):
            add_cross(at, block, HIGH_FAR, GROUP_FAR, place, z_re, z_im, z_sum, total)
            return carry

        lax.fori_loop(0, 16, turn, 0)
        settle(total, later)

    @pl.when(step == 0)
    def _():
        fetch.wait()

    lag_all()

    @pl.when(step < 3)
    def _():
        now[...] = later[...]


def correlations(place, blocks, before, mine, other):
    last = lambda j: jnp.minimum(j, 2)
    return pl.pallas_call(
        far_kernel,
        out_shape=jax.ShapeDtypeStruct((16, 2, 4, 8, LAGS), jnp.bfloat16),
        grid_spec=pltpu.PrefetchScalarGridSpec(
            num_scalar_prefetch=1,
            grid=(4,),
            in_specs=[
                pl.BlockSpec(BLOCK, lambda j, place: (last(j), 0, 0, 0, 0)),
                pl.BlockSpec((4, *TOTAL[1:]), lambda j, place: (0, 0, 0, 0, 0)),
                WHOLE,
                WHOLE,
                pl.BlockSpec(memory_space=pl.ANY),
            ],
            out_specs=pl.BlockSpec((16, 2, 1, 8, LAGS), lambda j, place: (0, 0, place[j], 0, 0)),
            scratch_shapes=[
                *ROW_SCRATCH,
                pltpu.VMEM(TOTAL[1:], jnp.float32),
                pltpu.VMEM((256, 2 * BINS), jnp.bfloat16),
                pltpu.VMEM((256, 2 * BINS), jnp.bfloat16),
                pltpu.VMEM((2 * BINS, LAGS_PAD), jnp.bfloat16),
                pltpu.SemaphoreType.DMA(()),
            ],
        ),
        compiler_params=pltpu.CompilerParams(vmem_limit_bytes=48 * 1024 * 1024),
        cost_estimate=pl.CostEstimate(
            flops=2 * 1024 * 1024 * LAGS, bytes_accessed=24 * 2**20, transcendentals=0
        ),
    )(place, blocks, before, mine, other, lag_table())


def shards(record, window_weight):
    plain, weighted = whiten(record, window_weight)
    z_low = lax.axis_index("win")
    row = lax.axis_index("row")
    col = lax.axis_index("col")
    x, z = row % 4, (row // 4) * 4 + z_low
    near_z = (z + jnp.array(NEAR)) % 8
    far_z = (z + jnp.array(FAR)) % 8
    place = jnp.concatenate(
        [
            (x + jnp.array([0, -1, 1, 2])) % 4,
            near_z // 4,
            near_z % 4,
            far_z // 4,
            far_z % 4,
            (col // 2 + (2 * (col % 2) + jnp.arange(4))) % 4,
            jnp.stack([col % 2]),
        ]
    ).astype(jnp.int32)
    arrived = first_step(plain, weighted)
    near, far, left, right, across, mine, other = second_step(plain, arrived)
    rest = third_step(far, across)
    before = near_totals(place, jnp.stack([near, far, left, right, across]), mine, other)
    corr = correlations(place, rest, before, mine, other)
    return corr.reshape(1, 1, 16, 8, 8, LAGS)


def solution(mesh):
    placed = (P("win", ("row", "col"), None), P("win"))
    return jax.shard_map(
        shards,
        mesh=mesh,
        in_specs=placed,
        out_specs=P("row", "win", None, None, "col", None),
        check_vma=False,
    )
```

```python
import math

import jax
import jax.numpy as jnp
import ml_dtypes
import numpy as np
from jax import lax
from jax.experimental import pallas as pl
from jax.experimental.pallas import tpu as pltpu
from jax.sharding import PartitionSpec as P

SAMPLES = 12000
QUARTER = 3000
BINS = 512
LAGS = 4000
LAGS_PAD = 4096
FIRST_BIN = 60
SMOOTH = 64
AXES = ("win", "row", "col")
BINS_AT = np.concatenate([np.arange(0, 512, 4), np.arange(2, 512, 4), np.arange(1, 512, 2)])
PHASE = 2.0 * np.pi / SAMPLES


def bf16(values):
    return values.astype(np.float32).astype(ml_dtypes.bfloat16)


def time_taper():
    index = np.arange(SAMPLES)
    edge = np.minimum(index, SAMPLES - 1 - index).astype(np.float64)
    ramp = max(SAMPLES // 20, 1)
    return np.where(edge < ramp, 0.5 - 0.5 * np.cos(np.pi * (edge + 0.5) / ramp), 1.0).astype(
        np.float32
    )


def band_taper():
    index = np.arange(BINS)
    edge = np.minimum(index, BINS - 1 - index).astype(np.float64)
    ramp = max(BINS // 16, 1)
    return np.where(edge < ramp, 0.5 - 0.5 * np.cos(np.pi * (edge + 1.0) / (ramp + 1.0)), 1.0).astype(
        np.float32
    )


def waves(bins):
    angle = PHASE * np.mod(np.arange(QUARTER)[:, None] * (bins + FIRST_BIN)[None, :], SAMPLES)
    return np.cos(angle), np.sin(angle)


def even_table(bins):
    cos, sin = waves(bins)
    return bf16(np.concatenate([cos, -sin], axis=1))


def odd_table(bins):
    cos, sin = waves(bins)
    turn = np.where((bins + FIRST_BIN) % 4 == 1, 1.0, -1.0)[None, :]
    first = np.concatenate([cos, -sin], axis=1)
    second = np.concatenate([-turn * sin, -turn * cos], axis=1)
    return bf16(np.concatenate([first, second], axis=0))


def lag_table():
    shifts = np.arange(LAGS) - LAGS // 2
    angle = PHASE * np.mod((BINS_AT + FIRST_BIN)[:, None] * shifts[None, :], SAMPLES)
    table = np.zeros((2 * BINS, LAGS_PAD))
    table[:BINS, :LAGS] = np.cos(angle)
    table[BINS:, :LAGS] = -np.sin(angle)
    return bf16(table / 128.0)


def smoother():
    index = np.arange(BINS)
    inside = (np.abs(index[:, None] - index[None, :]) <= SMOOTH).astype(np.float32)
    mean = inside / np.sum(inside, axis=0, keepdims=True, dtype=np.float32)
    return mean[BINS_AT][:, BINS_AT]


def whiten(record, weights):
    windows, channels, length = record.shape
    values = record.reshape(windows * channels, length).astype(jnp.float32)
    centered = (values - jnp.mean(values, axis=1, keepdims=True)) * time_taper()[None, :]
    centered = centered.astype(jnp.bfloat16).astype(jnp.float32)
    part = [centered[:, QUARTER * q : QUARTER * (q + 1)] for q in range(4)]
    sum02, dif02 = part[0] + part[2], part[0] - part[2]
    sum13, dif13 = part[1] + part[3], part[1] - part[3]
    even0 = (sum02 + sum13).astype(jnp.bfloat16)
    even2 = (sum02 - sum13).astype(jnp.bfloat16)
    odd = jnp.concatenate([dif02, dif13], axis=1).astype(jnp.bfloat16)

    def product(left, table):
        return jnp.dot(left, table, preferred_element_type=jnp.float32)

    spec0 = product(even0, even_table(BINS_AT[:128]))
    spec2 = product(even2, even_table(BINS_AT[128:256]))
    spec1 = product(odd, odd_table(BINS_AT[256:]))
    scale = 1.0 / math.sqrt(length)
    real_part = jnp.concatenate([spec0[:, :128], spec2[:, :128], spec1[:, :256]], axis=1) * scale
    imag_part = jnp.concatenate([spec0[:, 128:], spec2[:, 128:], spec1[:, 256:]], axis=1) * scale
    power = real_part * real_part + imag_part * imag_part
    smoothed = jnp.dot(
        power,
        smoother(),
        precision=lax.Precision.HIGHEST,
        preferred_element_type=jnp.float32,
    )
    gain = band_taper()[BINS_AT][None, :] / jnp.sqrt(smoothed + 1e-05)
    whitened = jnp.concatenate([real_part * gain, imag_part * gain], axis=1)
    whitened = whitened.reshape(windows, channels, 2 * BINS)
    plain = whitened.astype(jnp.bfloat16)
    weighted = (whitened * weights[:, None, None]).astype(jnp.bfloat16)
    return plain, weighted


def device_at(x, y, z, core):
    return ((z % 4) * 8 + (z // 4) * 4 + x) * 8 + y * 2 + core


def shift(value, dx=0, dy=0, dz=0, dcore=0):
    pairs = [
        (
            device_at(x, y, z, core),
            device_at((x + dx) % 4, (y + dy) % 4, (z + dz) % 8, (core + dcore) % 2),
        )
        for x in range(4)
        for y in range(4)
        for z in range(8)
        for core in range(2)
    ]
    return lax.ppermute(value, AXES, pairs)


def own_only(value, k):
    return lax.ppermute(value, "win", [(i, (i + k) % 4) for i in range(4)])


def together(*values):
    return lax.optimization_barrier(values)


def first_step(plain, weighted):
    return together(
        shift(plain, dz=4),
        shift(plain, dx=2),
        shift(plain, dz=1),
        shift(plain, dz=-1),
        shift(weighted, dy=1),
        shift(weighted, dy=2),
        shift(weighted, dy=3),
    )


def second_step(plain, weighted, arrived, y, z_low):
    opposite, across, below, above, *sides = arrived
    near = jnp.stack([plain, below, above, opposite])
    held = [weighted, *sides]

    def for_offset(k):
        at = (y - z_low - k) % 4
        low = jnp.where(at == 0, held[0], held[1])
        high = jnp.where(at == 2, held[2], held[3])
        return jnp.where(at < 2, low, high)

    mine = jnp.stack([for_offset(0)] + [own_only(for_offset(k), k) for k in (1, 2, 3)])
    return near, together(
        mine,
        shift(mine, dcore=1),
        shift(near, dx=1),
        shift(near, dx=-1),
        shift(jnp.stack([below, opposite, across]), dz=1),
        shift(jnp.stack([above, opposite, across]), dz=-1),
        shift(opposite, dx=2),
    )


def repack_kernel(up, down, across_opposite, far, up_out, down_out, done):
    pairs = (
        (up.at[0:2], far.at[0:2]),
        (down.at[0:2], far.at[2:4]),
        (up.at[2], up_out.at[0]),
        (across_opposite, up_out.at[1]),
        (down.at[2], down_out.at[0]),
        (across_opposite, down_out.at[1]),
    )
    copies = [
        pltpu.make_async_copy(source, target, done.at[n])
        for n, (source, target) in enumerate(pairs)
    ]
    for copy in copies:
        copy.start()
    for copy in copies:
        copy.wait()


def third_step(up, down, across_opposite):
    block = up.shape[1:]
    far, up_out, down_out = pl.pallas_call(
        repack_kernel,
        out_shape=[jax.ShapeDtypeStruct((n, *block), jnp.bfloat16) for n in (4, 2, 2)],
        in_specs=[pl.BlockSpec(memory_space=pl.ANY)] * 3,
        out_specs=[pl.BlockSpec(memory_space=pl.ANY)] * 3,
        scratch_shapes=[pltpu.SemaphoreType.DMA((6,))],
    )(up, down, across_opposite)
    return together(
        shift(far, dx=1),
        shift(far, dx=-1),
        shift(up_out, dz=1),
        shift(down_out, dz=-1),
    )


NEAR = (0, -1, 1, 4)
FAR = (-2, 3, 2, -3)
XS, HIGH_NEAR, GROUP_NEAR, HIGH_FAR, GROUP_FAR, ROWS, CORE = 0, 4, 8, 12, 16, 20, 24


def load_rows(place, mine, other, z_re, z_im, z_sum):
    core = place[CORE]
    for k in range(4):
        group = place[ROWS + k]
        for ref, at in ((mine, core), (other, 1 - core)):
            for w in range(8):
                value = ref[k, w].astype(jnp.float32)
                re, im = value[:, :BINS], value[:, BINS:]
                for tile in range(4):
                    lanes = slice(tile * 128, tile * 128 + 128)
                    z_re[group * 8 + w, at, tile] = re[:, lanes]
                    z_im[group * 8 + w, at, tile] = im[:, lanes]
                    z_sum[group * 8 + w, at, tile] = re[:, lanes] + im[:, lanes]


def add_cross(tile, block, high, group, rows, total):
    z_re, z_im, z_sum = rows
    lane = pl.ds(pl.multiple_of(tile * 128, 128), 128)
    lane_im = pl.ds(pl.multiple_of(tile * 128 + BINS, 128), 128)
    for core, base in ((0, 0), (0, 4), (1, 0), (1, 4)):
        sums = [None] * 12
        for w in range(8):
            yr = block[w, :, lane].astype(jnp.float32)
            yi = block[w, :, lane_im].astype(jnp.float32)
            dif = yr - yi
            window = group * 8 + w
            for i in range(4):
                row = pl.ds(base + i, 8, stride=0)
                terms = (
                    z_re[window, core, tile, row, :] * yr,
                    z_im[window, core, tile, row, :] * yi,
                    z_sum[window, core, tile, row, :] * dif,
                )
                for m, term in enumerate(terms):
                    at = i * 3 + m
                    sums[at] = term if w == 0 else sums[at] + term
        for i in range(4):
            p, q, r = sums[i * 3 : i * 3 + 3]
            total[high, core * 8 + base + i, :, lane] += p + q
            total[high, core * 8 + base + i, :, lane_im] += r - p + q


def add_blocks(blocks, place, high_at, group_at, rows, total):
    def tile_step(tile, carry):
        for n, block in enumerate(blocks):
            add_cross(tile, block, place[high_at + n], place[group_at + n], rows, total)
        return carry

    lax.fori_loop(0, 4, tile_step, 0)


def settle(source, target):
    for i in range(16):
        rows = jnp.concatenate([source[0, i], source[1, i]], axis=0)
        target[pl.ds(i * 16, 16), :] = rows.astype(jnp.bfloat16)


def near_kernel(
    place, near, up, down, left, right, across, across_opposite, mine, other, own, total, z_re, z_im, z_sum, sums
):
    rows = (z_re, z_im, z_sum)
    load_rows(place, mine, other, *rows)
    sums[...] = jnp.zeros_like(sums)
    total[...] = jnp.zeros_like(total)
    add_blocks([near.at[n] for n in range(4)], place, HIGH_NEAR, GROUP_NEAR, rows, sums)
    far = [up.at[0], up.at[1], down.at[0], down.at[1]]
    add_blocks(far, place, HIGH_FAR, GROUP_FAR, rows, sums)
    settle(sums, own)
    sides = (
        [left.at[n] for n in range(4)],
        [right.at[n] for n in range(4)],
        [across, up.at[2], down.at[2], across_opposite],
    )
    for n, blocks in enumerate(sides):
        add_blocks(blocks, place, HIGH_NEAR, GROUP_NEAR, rows, total.at[n])


WHOLE = pl.BlockSpec(memory_space=pltpu.VMEM)
SCALARS = pl.BlockSpec(memory_space=pltpu.SMEM)
TOTAL = (2, 16, 8, 2 * BINS)
OWN = jax.ShapeDtypeStruct((256, 2 * BINS), jnp.bfloat16)
ROW_SCRATCH = [pltpu.VMEM((32, 2, 4, 8, 128), jnp.float32)] * 3


def near_totals(place, *blocks):
    return pl.pallas_call(
        near_kernel,
        out_shape=(OWN, jax.ShapeDtypeStruct((3, *TOTAL), jnp.float32)),
        in_specs=[SCALARS] + [WHOLE] * len(blocks),
        out_specs=(WHOLE, WHOLE),
        scratch_shapes=[*ROW_SCRATCH, pltpu.VMEM(TOTAL, jnp.float32)],
        compiler_params=pltpu.CompilerParams(vmem_limit_bytes=24 * 1024 * 1024),
        cost_estimate=pl.CostEstimate(
            flops=12 * 10**9, bytes_accessed=8 * 2**20, transcendentals=0
        ),
    )(place, *blocks)


def far_kernel(
    place, left, right, up, down, own, before, mine, other, source, out, z_re, z_im, z_sum, total, now, later, table, ready
):
    step = pl.program_id(0)
    fetch = pltpu.make_async_copy(source, table, ready)
    rows = (z_re, z_im, z_sum)

    @pl.when(step == 0)
    def _():
        fetch.start()
        load_rows(place, mine, other, *rows)
        now[...] = own[...]

    chunks = (
        [left.at[n] for n in range(4)],
        [right.at[n] for n in range(4)],
        [up.at[0], up.at[1], down.at[0], down.at[1]],
    )
    for n, blocks in enumerate(chunks):

        @pl.when(step == n)
        def _():
            total[...] = before[0]
            add_blocks(blocks, place, HIGH_FAR, GROUP_FAR, rows, total)
            settle(total, later)

    @pl.when(step == 0)
    def _():
        fetch.wait()

    for tile in range(8):
        start = tile * 512
        keep = min(512, LAGS - start)
        value = jnp.dot(
            now[...], table[:, start : start + 512], preferred_element_type=jnp.float32
        )
        value = value.reshape(16, 2, 1, 8, 512).astype(jnp.bfloat16)
        out[:, :, :, :, start : start + keep] = value[..., :keep]

    @pl.when(step < 3)
    def _():
        now[...] = later[...]


def correlations(place, left, right, up, down, own, before, mine, other):
    return pl.pallas_call(
        far_kernel,
        out_shape=jax.ShapeDtypeStruct((16, 2, 4, 8, LAGS), jnp.bfloat16),
        grid_spec=pltpu.PrefetchScalarGridSpec(
            num_scalar_prefetch=1,
            grid=(4,),
            in_specs=[
                WHOLE,
                WHOLE,
                WHOLE,
                WHOLE,
                WHOLE,
                pl.BlockSpec((1, *TOTAL), lambda j, place: (jnp.minimum(j, 2), 0, 0, 0, 0)),
                WHOLE,
                WHOLE,
                pl.BlockSpec(memory_space=pl.ANY),
            ],
            out_specs=pl.BlockSpec((16, 2, 1, 8, LAGS), lambda j, place: (0, 0, place[j], 0, 0)),
            scratch_shapes=[
                *ROW_SCRATCH,
                pltpu.VMEM(TOTAL, jnp.float32),
                pltpu.VMEM((256, 2 * BINS), jnp.bfloat16),
                pltpu.VMEM((256, 2 * BINS), jnp.bfloat16),
                pltpu.VMEM((2 * BINS, LAGS_PAD), jnp.bfloat16),
                pltpu.SemaphoreType.DMA(()),
            ],
        ),
        compiler_params=pltpu.CompilerParams(vmem_limit_bytes=32 * 1024 * 1024),
        cost_estimate=pl.CostEstimate(
            flops=2 * 1024 * 1024 * LAGS, bytes_accessed=24 * 2**20, transcendentals=0
        ),
    )(place, left, right, up, down, own, before, mine, other, lag_table())


def shards(record, window_weight):
    plain, weighted = whiten(record, window_weight)
    z_low = lax.axis_index("win")
    row = lax.axis_index("row")
    col = lax.axis_index("col")
    x, z = row % 4, (row // 4) * 4 + z_low
    near_z = (z + jnp.array(NEAR)) % 8
    far_z = (z + jnp.array(FAR)) % 8
    place = jnp.concatenate(
        [
            (x + jnp.array([0, -1, 1, 2])) % 4,
            near_z // 4,
            near_z % 4,
            far_z // 4,
            far_z % 4,
            (z_low - jnp.arange(4)) % 4,
            jnp.stack([col % 2]),
        ]
    ).astype(jnp.int32)
    arrived = first_step(plain, weighted)
    near, sent = second_step(plain, weighted, arrived, col // 2, z_low)
    mine, other, left, right, up, down, across_opposite = sent
    rest = third_step(up, down, across_opposite)
    own, before = near_totals(
        place, near, up, down, left, right, arrived[1], across_opposite, mine, other
    )
    corr = correlations(place, *rest, own, before, mine, other)
    return corr.reshape(1, 1, 16, 8, 8, LAGS)


def solution(mesh):
    placed = (P("win", ("row", "col"), None), P("win"))
    return jax.shard_map(
        shards,
        mesh=mesh,
        in_specs=placed,
        out_specs=P("row", "win", None, None, "col", None),
        check_vma=False,
    )
```

```python
import math

import jax
import jax.numpy as jnp
import ml_dtypes
import numpy as np
from jax import lax
from jax.experimental import pallas as pl
from jax.experimental.pallas import tpu as pltpu
from jax.sharding import PartitionSpec as P

SAMPLES = 12000
QUARTER = 3000
BINS = 512
LAGS = 4000
LAGS_PAD = 4096
FIRST_BIN = 60
SMOOTH = 64
AXES = ("win", "row", "col")
BINS_AT = np.concatenate([np.arange(0, 512, 4), np.arange(2, 512, 4), np.arange(1, 512, 2)])
PHASE = 2.0 * np.pi / SAMPLES


def bf16(values):
    return values.astype(np.float32).astype(ml_dtypes.bfloat16)


def time_taper():
    index = np.arange(SAMPLES)
    edge = np.minimum(index, SAMPLES - 1 - index).astype(np.float64)
    ramp = max(SAMPLES // 20, 1)
    return np.where(edge < ramp, 0.5 - 0.5 * np.cos(np.pi * (edge + 0.5) / ramp), 1.0).astype(
        np.float32
    )


def band_taper():
    index = np.arange(BINS)
    edge = np.minimum(index, BINS - 1 - index).astype(np.float64)
    ramp = max(BINS // 16, 1)
    return np.where(edge < ramp, 0.5 - 0.5 * np.cos(np.pi * (edge + 1.0) / (ramp + 1.0)), 1.0).astype(
        np.float32
    )


def waves(bins):
    angle = PHASE * np.mod(np.arange(QUARTER)[:, None] * (bins + FIRST_BIN)[None, :], SAMPLES)
    return np.cos(angle), np.sin(angle)


def even_table(bins):
    cos, sin = waves(bins)
    return bf16(np.concatenate([cos, -sin], axis=1))


def odd_table(bins):
    cos, sin = waves(bins)
    turn = np.where((bins + FIRST_BIN) % 4 == 1, 1.0, -1.0)[None, :]
    first = np.concatenate([cos, -sin], axis=1)
    second = np.concatenate([-turn * sin, -turn * cos], axis=1)
    return bf16(np.concatenate([first, second], axis=0))


def lag_table():
    shifts = np.arange(LAGS) - LAGS // 2
    angle = PHASE * np.mod((BINS_AT + FIRST_BIN)[:, None] * shifts[None, :], SAMPLES)
    table = np.zeros((2 * BINS, LAGS_PAD))
    table[:BINS, :LAGS] = np.cos(angle)
    table[BINS:, :LAGS] = -np.sin(angle)
    return bf16(table / 128.0)


def smoother():
    index = np.arange(BINS)
    inside = (np.abs(index[:, None] - index[None, :]) <= SMOOTH).astype(np.float32)
    mean = inside / np.sum(inside, axis=0, keepdims=True, dtype=np.float32)
    return mean[BINS_AT][:, BINS_AT]


def whiten(record, weights):
    windows, channels, length = record.shape
    values = record.reshape(windows * channels, length).astype(jnp.float32)
    centered = (values - jnp.mean(values, axis=1, keepdims=True)) * time_taper()[None, :]
    centered = centered.astype(jnp.bfloat16).astype(jnp.float32)
    part = [centered[:, QUARTER * q : QUARTER * (q + 1)] for q in range(4)]
    sum02, dif02 = part[0] + part[2], part[0] - part[2]
    sum13, dif13 = part[1] + part[3], part[1] - part[3]
    even0 = (sum02 + sum13).astype(jnp.bfloat16)
    even2 = (sum02 - sum13).astype(jnp.bfloat16)
    odd = jnp.concatenate([dif02, dif13], axis=1).astype(jnp.bfloat16)

    def product(left, table):
        return jnp.dot(left, table, preferred_element_type=jnp.float32)

    spec0 = product(even0, even_table(BINS_AT[:128]))
    spec2 = product(even2, even_table(BINS_AT[128:256]))
    spec1 = product(odd, odd_table(BINS_AT[256:]))
    scale = 1.0 / math.sqrt(length)
    real_part = jnp.concatenate([spec0[:, :128], spec2[:, :128], spec1[:, :256]], axis=1) * scale
    imag_part = jnp.concatenate([spec0[:, 128:], spec2[:, 128:], spec1[:, 256:]], axis=1) * scale
    power = real_part * real_part + imag_part * imag_part
    smoothed = jnp.dot(
        power,
        smoother(),
        precision=lax.Precision.HIGHEST,
        preferred_element_type=jnp.float32,
    )
    gain = band_taper()[BINS_AT][None, :] / jnp.sqrt(smoothed + 1e-05)
    whitened = jnp.concatenate([real_part * gain, imag_part * gain], axis=1)
    whitened = whitened.reshape(windows, channels, 2 * BINS)
    plain = whitened.astype(jnp.bfloat16)
    weighted = (whitened * weights[:, None, None]).astype(jnp.bfloat16)
    return plain, weighted


def device_at(x, y, z, core):
    return ((z % 4) * 8 + (z // 4) * 4 + x) * 8 + y * 2 + core


def shift(value, dx=0, dy=0, dz=0, dcore=0):
    pairs = [
        (
            device_at(x, y, z, core),
            device_at((x + dx) % 4, (y + dy) % 4, (z + dz) % 8, (core + dcore) % 2),
        )
        for x in range(4)
        for y in range(4)
        for z in range(8)
        for core in range(2)
    ]
    return lax.ppermute(value, AXES, pairs)


def own_only(value, k):
    return lax.ppermute(value, "win", [(i, (i + k) % 4) for i in range(4)])


def together(*values):
    return lax.optimization_barrier(values)


def first_step(plain, weighted):
    return together(
        shift(plain, dz=-3),
        shift(plain, dz=2),
        shift(plain, dx=2),
        shift(weighted, dy=1),
        shift(weighted, dy=2),
        shift(weighted, dy=3),
    )


def second_step(plain, weighted, arrived, y, z_low):
    ahead, behind, across, *sides = arrived
    near = jnp.stack([plain, ahead, behind])
    held = [weighted, *sides]

    def for_offset(k):
        at = (y - z_low - k) % 4
        low = jnp.where(at == 0, held[0], held[1])
        high = jnp.where(at == 2, held[2], held[3])
        return jnp.where(at < 2, low, high)

    mine = jnp.stack([for_offset(0)] + [own_only(for_offset(k), k) for k in (1, 2, 3)])
    return near, together(
        mine,
        shift(mine, dcore=1),
        shift(near, dx=1),
        shift(near, dx=-1),
        shift(near, dz=1),
        shift(jnp.stack([plain, ahead]), dz=-1),
        shift(jnp.stack([ahead, behind]), dx=2),
    )


def third_step(up, down, across, across_near):
    far = jnp.concatenate([up, down])
    return together(
        shift(far, dx=1),
        shift(far, dx=-1),
        shift(jnp.concatenate([across[None], across_near]), dz=1),
        shift(jnp.stack([across, across_near[0]]), dz=-1),
    )


NEAR = (0, 3, -2)
FAR = (-1, 2, -3, 1, 4)
XS, HIGH, GROUP, ROWS, CORE = 0, 4, 12, 20, 24


def load_rows(place, mine, other, z_re, z_im, z_sum):
    core = place[CORE]
    for k in range(4):
        group = place[ROWS + k]
        for ref, at in ((mine, core), (other, 1 - core)):
            for w in range(8):
                value = ref[k, w].astype(jnp.float32)
                re, im = value[:, :BINS], value[:, BINS:]
                for tile in range(4):
                    lanes = slice(tile * 128, tile * 128 + 128)
                    z_re[group * 8 + w, at, tile] = re[:, lanes]
                    z_im[group * 8 + w, at, tile] = im[:, lanes]
                    z_sum[group * 8 + w, at, tile] = re[:, lanes] + im[:, lanes]


def add_cross(tile, block, high, group, rows, total):
    z_re, z_im, z_sum = rows
    lane = pl.ds(pl.multiple_of(tile * 128, 128), 128)
    lane_im = pl.ds(pl.multiple_of(tile * 128 + BINS, 128), 128)
    for core, base in ((0, 0), (0, 4), (1, 0), (1, 4)):
        sums = [None] * 12
        for w in range(8):
            yr = block[w, :, lane].astype(jnp.float32)
            yi = block[w, :, lane_im].astype(jnp.float32)
            dif = yr - yi
            window = group * 8 + w
            for i in range(4):
                row = pl.ds(base + i, 8, stride=0)
                terms = (
                    z_re[window, core, tile, row, :] * yr,
                    z_im[window, core, tile, row, :] * yi,
                    z_sum[window, core, tile, row, :] * dif,
                )
                for m, term in enumerate(terms):
                    at = i * 3 + m
                    sums[at] = term if w == 0 else sums[at] + term
        for i in range(4):
            p, q, r = sums[i * 3 : i * 3 + 3]
            total[high, core * 8 + base + i, :, lane] += p + q
            total[high, core * 8 + base + i, :, lane_im] += r - p + q


def add_blocks(blocks, place, first, rows, total):
    def tile_step(tile, carry):
        for n, block in enumerate(blocks, first):
            add_cross(tile, block, place[HIGH + n], place[GROUP + n], rows, total)
        return carry

    lax.fori_loop(0, 4, tile_step, 0)


def settle(source, target):
    for i in range(16):
        rows = jnp.concatenate([source[0, i], source[1, i]], axis=0)
        target[pl.ds(i * 16, 16), :] = rows.astype(jnp.bfloat16)


def parts_of(*refs):
    return [ref.at[n] for ref in refs for n in range(ref.shape[0])]


def near_kernel(
    place, near, up, down, left, right, across, across_near, mine, other, own, total, z_re, z_im, z_sum, sums
):
    rows = (z_re, z_im, z_sum)
    load_rows(place, mine, other, *rows)
    sums[...] = jnp.zeros_like(sums)
    total[...] = jnp.zeros_like(total)
    add_blocks(parts_of(near, up, down), place, 0, rows, sums)
    settle(sums, own)
    sides = (parts_of(left), parts_of(right), [across, *parts_of(across_near)])
    for n, blocks in enumerate(sides):
        add_blocks(blocks, place, 0, rows, total.at[n])


TOTAL = (2, 16, 8, 2 * BINS)
OWN = (256, 2 * BINS)
ROW_SCRATCH = [pltpu.VMEM((32, 2, 4, 8, 128), jnp.float32)] * 3


def whole(shape):
    return pl.BlockSpec(shape, lambda j, place: (0,) * len(shape))


def near_totals(place, *blocks):
    return pl.pallas_call(
        near_kernel,
        out_shape=(
            jax.ShapeDtypeStruct(OWN, jnp.bfloat16),
            jax.ShapeDtypeStruct((3, *TOTAL), jnp.float32),
        ),
        grid_spec=pltpu.PrefetchScalarGridSpec(
            num_scalar_prefetch=1,
            grid=(1,),
            in_specs=[whole(block.shape) for block in blocks],
            out_specs=(whole(OWN), whole((3, *TOTAL))),
            scratch_shapes=[*ROW_SCRATCH, pltpu.VMEM(TOTAL, jnp.float32)],
        ),
        compiler_params=pltpu.CompilerParams(vmem_limit_bytes=28 * 1024 * 1024),
        cost_estimate=pl.CostEstimate(
            flops=12 * 10**9, bytes_accessed=8 * 2**20, transcendentals=0
        ),
    )(place, *blocks)


def far_kernel(
    place, left, right, up, down, own, before, mine, other, source, out, z_re, z_im, z_sum, total, now, later, table, ready
):
    step = pl.program_id(0)
    fetch = pltpu.make_async_copy(source, table, ready)
    rows = (z_re, z_im, z_sum)

    @pl.when(step == 0)
    def _():
        fetch.start()
        load_rows(place, mine, other, *rows)
        now[...] = own[...]

    chunks = (parts_of(left), parts_of(right), parts_of(up, down))
    for n, blocks in enumerate(chunks):

        @pl.when(step == n)
        def _():
            total[...] = before[0]
            add_blocks(blocks, place, 3, rows, total)
            settle(total, later)

    @pl.when(step == 0)
    def _():
        fetch.wait()

    for tile in range(8):
        start = tile * 512
        keep = min(512, LAGS - start)
        value = jnp.dot(
            now[...], table[:, start : start + 512], preferred_element_type=jnp.float32
        )
        value = value.reshape(16, 2, 1, 8, 512).astype(jnp.bfloat16)
        out[:, :, :, :, start : start + keep] = value[..., :keep]

    @pl.when(step < 3)
    def _():
        now[...] = later[...]


def correlations(place, left, right, up, down, own, before, mine, other):
    return pl.pallas_call(
        far_kernel,
        out_shape=jax.ShapeDtypeStruct((16, 2, 4, 8, LAGS), jnp.bfloat16),
        grid_spec=pltpu.PrefetchScalarGridSpec(
            num_scalar_prefetch=1,
            grid=(4,),
            in_specs=[
                *[whole(block.shape) for block in (left, right, up, down, own)],
                pl.BlockSpec((1, *TOTAL), lambda j, place: (jnp.minimum(j, 2), 0, 0, 0, 0)),
                *[whole(block.shape) for block in (mine, other)],
                pl.BlockSpec(memory_space=pl.ANY),
            ],
            out_specs=pl.BlockSpec((16, 2, 1, 8, LAGS), lambda j, place: (0, 0, place[j], 0, 0)),
            scratch_shapes=[
                *ROW_SCRATCH,
                pltpu.VMEM(TOTAL, jnp.float32),
                pltpu.VMEM((256, 2 * BINS), jnp.bfloat16),
                pltpu.VMEM((256, 2 * BINS), jnp.bfloat16),
                pltpu.VMEM((2 * BINS, LAGS_PAD), jnp.bfloat16),
                pltpu.SemaphoreType.DMA(()),
            ],
        ),
        compiler_params=pltpu.CompilerParams(vmem_limit_bytes=36 * 1024 * 1024),
        cost_estimate=pl.CostEstimate(
            flops=2 * 1024 * 1024 * LAGS, bytes_accessed=24 * 2**20, transcendentals=0
        ),
    )(place, left, right, up, down, own, before, mine, other, lag_table())


def shards(record, window_weight):
    plain, weighted = whiten(record, window_weight)
    z_low = lax.axis_index("win")
    row = lax.axis_index("row")
    col = lax.axis_index("col")
    x, z = row % 4, (row // 4) * 4 + z_low
    where = (z + jnp.array(NEAR + FAR)) % 8
    place = jnp.concatenate(
        [
            (x + jnp.array([0, -1, 1, 2])) % 4,
            where // 4,
            where % 4,
            (z_low - jnp.arange(4)) % 4,
            jnp.stack([col % 2]),
        ]
    ).astype(jnp.int32)
    arrived = first_step(plain, weighted)
    near, sent = second_step(plain, weighted, arrived, col // 2, z_low)
    mine, other, left, right, up, down, across_near = sent
    across = arrived[2]
    rest = third_step(up, down, across, across_near)
    own, before = near_totals(
        place, near, up, down, left, right, across, across_near, mine, other
    )
    corr = correlations(place, *rest, own, before, mine, other)
    return corr.reshape(1, 1, 16, 8, 8, LAGS)


def solution(mesh):
    placed = (P("win", ("row", "col"), None), P("win"))
    return jax.shard_map(
        shards,
        mesh=mesh,
        in_specs=placed,
        out_specs=P("row", "win", None, None, "col", None),
        check_vma=False,
    )
```

```python
import math

import jax
import jax.numpy as jnp
import ml_dtypes
import numpy as np
from jax import lax
from jax.experimental import pallas as pl
from jax.experimental.pallas import tpu as pltpu
from jax.sharding import PartitionSpec as P

SAMPLES = 12000
QUARTER = 3000
BINS = 512
LAGS = 4000
LAGS_PAD = 4096
FIRST_BIN = 60
SMOOTH = 64
AXES = ("win", "row", "col")
BINS_AT = np.concatenate([np.arange(0, 512, 4), np.arange(2, 512, 4), np.arange(1, 512, 2)])
PHASE = 2.0 * np.pi / SAMPLES


def bf16(values):
    return values.astype(np.float32).astype(ml_dtypes.bfloat16)


def time_taper():
    index = np.arange(SAMPLES)
    edge = np.minimum(index, SAMPLES - 1 - index).astype(np.float64)
    ramp = max(SAMPLES // 20, 1)
    return np.where(edge < ramp, 0.5 - 0.5 * np.cos(np.pi * (edge + 0.5) / ramp), 1.0).astype(
        np.float32
    )


def band_taper():
    index = np.arange(BINS)
    edge = np.minimum(index, BINS - 1 - index).astype(np.float64)
    ramp = max(BINS // 16, 1)
    return np.where(edge < ramp, 0.5 - 0.5 * np.cos(np.pi * (edge + 1.0) / (ramp + 1.0)), 1.0).astype(
        np.float32
    )


def waves(bins):
    angle = PHASE * np.mod(np.arange(QUARTER)[:, None] * (bins + FIRST_BIN)[None, :], SAMPLES)
    return np.cos(angle), np.sin(angle)


def even_table(bins):
    cos, sin = waves(bins)
    return bf16(np.concatenate([cos, -sin], axis=1))


def odd_table(bins):
    cos, sin = waves(bins)
    turn = np.where((bins + FIRST_BIN) % 4 == 1, 1.0, -1.0)[None, :]
    first = np.concatenate([cos, -sin], axis=1)
    second = np.concatenate([-turn * sin, -turn * cos], axis=1)
    return bf16(np.concatenate([first, second], axis=0))


def lag_table():
    shifts = np.arange(LAGS) - LAGS // 2
    angle = PHASE * np.mod((BINS_AT + FIRST_BIN)[:, None] * shifts[None, :], SAMPLES)
    table = np.zeros((2 * BINS, LAGS_PAD))
    table[:BINS, :LAGS] = np.cos(angle)
    table[BINS:, :LAGS] = -np.sin(angle)
    return bf16(table / 128.0)


def smoother():
    index = np.arange(BINS)
    inside = (np.abs(index[:, None] - index[None, :]) <= SMOOTH).astype(np.float32)
    mean = inside / np.sum(inside, axis=0, keepdims=True, dtype=np.float32)
    return mean[BINS_AT][:, BINS_AT]


def whiten(record, weights):
    windows, channels, length = record.shape
    values = record.reshape(windows * channels, length).astype(jnp.float32)
    centered = (values - jnp.mean(values, axis=1, keepdims=True)) * time_taper()[None, :]
    centered = centered.astype(jnp.bfloat16).astype(jnp.float32)
    part = [centered[:, QUARTER * q : QUARTER * (q + 1)] for q in range(4)]
    sum02, dif02 = part[0] + part[2], part[0] - part[2]
    sum13, dif13 = part[1] + part[3], part[1] - part[3]
    even0 = (sum02 + sum13).astype(jnp.bfloat16)
    even2 = (sum02 - sum13).astype(jnp.bfloat16)
    odd = jnp.concatenate([dif02, dif13], axis=1).astype(jnp.bfloat16)

    def product(left, table):
        return jnp.dot(left, table, preferred_element_type=jnp.float32)

    spec0 = product(even0, even_table(BINS_AT[:128]))
    spec2 = product(even2, even_table(BINS_AT[128:256]))
    spec1 = product(odd, odd_table(BINS_AT[256:]))
    scale = 1.0 / math.sqrt(length)
    real_part = jnp.concatenate([spec0[:, :128], spec2[:, :128], spec1[:, :256]], axis=1) * scale
    imag_part = jnp.concatenate([spec0[:, 128:], spec2[:, 128:], spec1[:, 256:]], axis=1) * scale
    power = real_part * real_part + imag_part * imag_part
    smoothed = jnp.dot(
        power,
        smoother(),
        precision=lax.Precision.HIGHEST,
        preferred_element_type=jnp.float32,
    )
    gain = band_taper()[BINS_AT][None, :] / jnp.sqrt(smoothed + 1e-05)
    whitened = jnp.concatenate([real_part * gain, imag_part * gain], axis=1)
    whitened = whitened.reshape(windows, channels, 2 * BINS)
    plain = whitened.astype(jnp.bfloat16)
    weighted = (whitened * weights[:, None, None]).astype(jnp.bfloat16)
    return plain, weighted


def device_at(x, y, z, core):
    return ((z % 4) * 8 + (z // 4) * 4 + x) * 8 + y * 2 + core


def shift(value, dx=0, dy=0, dz=0, dcore=0):
    pairs = [
        (
            device_at(x, y, z, core),
            device_at((x + dx) % 4, (y + dy) % 4, (z + dz) % 8, (core + dcore) % 2),
        )
        for x in range(4)
        for y in range(4)
        for z in range(8)
        for core in range(2)
    ]
    return lax.ppermute(value, AXES, pairs)


def own_only(value, k):
    return lax.ppermute(value, "win", [(i, (i + k) % 4) for i in range(4)])


def together(*values):
    return lax.optimization_barrier(values)


def first_step(plain, weighted):
    return together(
        shift(weighted, dy=1),
        shift(weighted, dy=3),
        shift(weighted, dy=2),
        shift(plain, dx=2),
        shift(plain, dz=2),
        shift(plain, dz=-3),
    )


def second_step(plain, weighted, arrived, y, z_low):
    left, right, opposite, across, behind, ahead = arrived
    near = jnp.stack([plain, ahead, behind])
    held = [weighted, left, opposite, right]

    def for_offset(k):
        at = (y - z_low - k) % 4
        low = jnp.where(at == 0, held[0], held[1])
        high = jnp.where(at == 2, held[2], held[3])
        return jnp.where(at < 2, low, high)

    return together(
        for_offset(0),
        own_only(for_offset(1), 1),
        own_only(for_offset(2), 2),
        own_only(for_offset(3), 3),
        shift(near, dx=-1),
        shift(near, dx=1),
        near,
        across,
    )


def third_step(arrived):
    *rows, right, left, near, across = arrived
    mine = jnp.stack(rows)
    across_near, other, down, up, *rest = together(
        shift(near[1:], dx=2),
        shift(mine, dcore=1),
        shift(near[:2], dz=-1),
        shift(near, dz=1),
        mine,
        near,
        left,
        right,
        across,
    )
    mine, near, left, right, across = rest
    return near, up, down, left, right, across, across_near, mine, other


def fourth_step(up, down, across, across_near):
    far = jnp.concatenate([up, down])
    down_out, up_out, right, left = together(
        shift(jnp.stack([across, across_near[0]]), dz=-1),
        shift(jnp.concatenate([across[None], across_near]), dz=1),
        shift(far, dx=-1),
        shift(far, dx=1),
    )
    return left, right, up_out, down_out


NEAR = (0, 3, -2)
FAR = (-1, 2, -3, 1, 4)
XS, HIGH, GROUP, ROWS, CORE = 0, 4, 12, 20, 24


def load_rows(place, mine, other, z_re, z_im, z_sum):
    core = place[CORE]
    for k in range(4):
        group = place[ROWS + k]
        for ref, at in ((mine, core), (other, 1 - core)):
            for w in range(8):
                value = ref[k, w].astype(jnp.float32)
                re, im = value[:, :BINS], value[:, BINS:]
                for tile in range(4):
                    lanes = slice(tile * 128, tile * 128 + 128)
                    z_re[group * 8 + w, at, tile] = re[:, lanes]
                    z_im[group * 8 + w, at, tile] = im[:, lanes]
                    z_sum[group * 8 + w, at, tile] = re[:, lanes] + im[:, lanes]


def add_cross(tile, block, high, group, rows, total):
    z_re, z_im, z_sum = rows
    lane = pl.ds(pl.multiple_of(tile * 128, 128), 128)
    lane_im = pl.ds(pl.multiple_of(tile * 128 + BINS, 128), 128)
    for core, base in ((0, 0), (0, 4), (1, 0), (1, 4)):
        sums = [None] * 12
        for w in range(8):
            yr = block[w, :, lane].astype(jnp.float32)
            yi = block[w, :, lane_im].astype(jnp.float32)
            dif = yr - yi
            window = group * 8 + w
            for i in range(4):
                row = pl.ds(base + i, 8, stride=0)
                terms = (
                    z_re[window, core, tile, row, :] * yr,
                    z_im[window, core, tile, row, :] * yi,
                    z_sum[window, core, tile, row, :] * dif,
                )
                for m, term in enumerate(terms):
                    at = i * 3 + m
                    sums[at] = term if w == 0 else sums[at] + term
        for i in range(4):
            p, q, r = sums[i * 3 : i * 3 + 3]
            total[high, core * 8 + base + i, :, lane] += p + q
            total[high, core * 8 + base + i, :, lane_im] += r - p + q


def add_blocks(blocks, place, first, rows, total):
    def tile_step(tile, carry):
        for n, block in enumerate(blocks, first):
            add_cross(tile, block, place[HIGH + n], place[GROUP + n], rows, total)
        return carry

    lax.fori_loop(0, 4, tile_step, 0)


def settle(source, target):
    for i in range(16):
        rows = jnp.concatenate([source[0, i], source[1, i]], axis=0)
        target[pl.ds(i * 16, 16), :] = rows.astype(jnp.bfloat16)


def parts_of(*refs):
    return [ref.at[n] for ref in refs for n in range(ref.shape[0])]


def near_kernel(
    place, near, up, down, left, right, across, across_near, mine, other, own, total, z_re, z_im, z_sum, sums
):
    rows = (z_re, z_im, z_sum)
    load_rows(place, mine, other, *rows)
    sums[...] = jnp.zeros_like(sums)
    total[...] = jnp.zeros_like(total)
    add_blocks(parts_of(near, up, down), place, 0, rows, sums)
    settle(sums, own)
    sides = (parts_of(left), parts_of(right), [across, *parts_of(across_near)])
    for n, blocks in enumerate(sides):
        add_blocks(blocks, place, 0, rows, total.at[n])


TOTAL = (2, 16, 8, 2 * BINS)
OWN = (256, 2 * BINS)
ROW_SCRATCH = [pltpu.VMEM((32, 2, 4, 8, 128), jnp.float32)] * 3


def whole(shape):
    return pl.BlockSpec(shape, lambda j, place: (0,) * len(shape))


def near_totals(place, *blocks):
    return pl.pallas_call(
        near_kernel,
        out_shape=(
            jax.ShapeDtypeStruct(OWN, jnp.bfloat16),
            jax.ShapeDtypeStruct((3, *TOTAL), jnp.float32),
        ),
        grid_spec=pltpu.PrefetchScalarGridSpec(
            num_scalar_prefetch=1,
            grid=(1,),
            in_specs=[whole(block.shape) for block in blocks],
            out_specs=(whole(OWN), whole((3, *TOTAL))),
            scratch_shapes=[*ROW_SCRATCH, pltpu.VMEM(TOTAL, jnp.float32)],
        ),
        compiler_params=pltpu.CompilerParams(vmem_limit_bytes=28 * 1024 * 1024),
        cost_estimate=pl.CostEstimate(
            flops=12 * 10**9, bytes_accessed=8 * 2**20, transcendentals=0
        ),
    )(place, *blocks)


def far_kernel(
    place, left, right, up, down, own, before, mine, other, source, out, z_re, z_im, z_sum, total, now, later, table, ready
):
    step = pl.program_id(0)
    fetch = pltpu.make_async_copy(source, table, ready)
    rows = (z_re, z_im, z_sum)

    @pl.when(step == 0)
    def _():
        fetch.start()
        load_rows(place, mine, other, *rows)
        now[...] = own[...]

    chunks = (parts_of(left), parts_of(right), parts_of(up, down))
    for n, blocks in enumerate(chunks):

        @pl.when(step == n)
        def _():
            total[...] = before[0]
            add_blocks(blocks, place, 3, rows, total)
            settle(total, later)

    @pl.when(step == 0)
    def _():
        fetch.wait()

    for tile in range(8):
        start = tile * 512
        keep = min(512, LAGS - start)
        value = jnp.dot(
            now[...], table[:, start : start + 512], preferred_element_type=jnp.float32
        )
        value = value.reshape(16, 2, 1, 8, 512).astype(jnp.bfloat16)
        out[:, :, :, :, start : start + keep] = value[..., :keep]

    @pl.when(step < 3)
    def _():
        now[...] = later[...]


def correlations(place, left, right, up, down, own, before, mine, other):
    return pl.pallas_call(
        far_kernel,
        out_shape=jax.ShapeDtypeStruct((16, 2, 4, 8, LAGS), jnp.bfloat16),
        grid_spec=pltpu.PrefetchScalarGridSpec(
            num_scalar_prefetch=1,
            grid=(4,),
            in_specs=[
                *[whole(block.shape) for block in (left, right, up, down, own)],
                pl.BlockSpec((1, *TOTAL), lambda j, place: (jnp.minimum(j, 2), 0, 0, 0, 0)),
                *[whole(block.shape) for block in (mine, other)],
                pl.BlockSpec(memory_space=pl.ANY),
            ],
            out_specs=pl.BlockSpec((16, 2, 1, 8, LAGS), lambda j, place: (0, 0, place[j], 0, 0)),
            scratch_shapes=[
                *ROW_SCRATCH,
                pltpu.VMEM(TOTAL, jnp.float32),
                pltpu.VMEM((256, 2 * BINS), jnp.bfloat16),
                pltpu.VMEM((256, 2 * BINS), jnp.bfloat16),
                pltpu.VMEM((2 * BINS, LAGS_PAD), jnp.bfloat16),
                pltpu.SemaphoreType.DMA(()),
            ],
        ),
        compiler_params=pltpu.CompilerParams(vmem_limit_bytes=36 * 1024 * 1024),
        cost_estimate=pl.CostEstimate(
            flops=2 * 1024 * 1024 * LAGS, bytes_accessed=24 * 2**20, transcendentals=0
        ),
    )(place, left, right, up, down, own, before, mine, other, lag_table())


def shards(record, window_weight):
    plain, weighted = whiten(record, window_weight)
    z_low = lax.axis_index("win")
    row = lax.axis_index("row")
    col = lax.axis_index("col")
    x, z = row % 4, (row // 4) * 4 + z_low
    where = (z + jnp.array(NEAR + FAR)) % 8
    place = jnp.concatenate(
        [
            (x + jnp.array([0, -1, 1, 2])) % 4,
            where // 4,
            where % 4,
            (z_low - jnp.arange(4)) % 4,
            jnp.stack([col % 2]),
        ]
    ).astype(jnp.int32)
    arrived = first_step(plain, weighted)
    arrived = second_step(plain, weighted, arrived, col // 2, z_low)
    near, up, down, left, right, across, across_near, mine, other = third_step(arrived)
    rest = fourth_step(up, down, across, across_near)
    own, before = near_totals(
        place, near, up, down, left, right, across, across_near, mine, other
    )
    corr = correlations(place, *rest, own, before, mine, other)
    return corr.reshape(1, 1, 16, 8, 8, LAGS)


def solution(mesh):
    placed = (P("win", ("row", "col"), None), P("win"))
    return jax.shard_map(
        shards,
        mesh=mesh,
        in_specs=placed,
        out_specs=P("row", "win", None, None, "col", None),
        check_vma=False,
    )
```

```python
import math

import jax
import jax.numpy as jnp
import ml_dtypes
import numpy as np
from jax import lax
from jax.experimental import pallas as pl
from jax.experimental.pallas import tpu as pltpu
from jax.sharding import PartitionSpec as P

SAMPLES = 12000
QUARTER = 3000
QUARTER_PAD = 3072
BINS = 512
LAGS = 4000
LAGS_PAD = 4096
FIRST_BIN = 60
SMOOTH = 64
AXES = ("win", "row", "col")
BINS_AT = np.concatenate([np.arange(0, 512, 4), np.arange(2, 512, 4), np.arange(1, 512, 2)])
PHASE = 2.0 * np.pi / SAMPLES


def bf16(values):
    return values.astype(np.float32).astype(ml_dtypes.bfloat16)


def time_taper():
    index = np.arange(SAMPLES)
    edge = np.minimum(index, SAMPLES - 1 - index).astype(np.float64)
    ramp = max(SAMPLES // 20, 1)
    return np.where(edge < ramp, 0.5 - 0.5 * np.cos(np.pi * (edge + 0.5) / ramp), 1.0).astype(
        np.float32
    )


def band_taper():
    index = np.arange(BINS)
    edge = np.minimum(index, BINS - 1 - index).astype(np.float64)
    ramp = max(BINS // 16, 1)
    return np.where(edge < ramp, 0.5 - 0.5 * np.cos(np.pi * (edge + 1.0) / (ramp + 1.0)), 1.0).astype(
        np.float32
    )


def padded(table):
    return bf16(np.pad(table, ((0, QUARTER_PAD - QUARTER), (0, 0))))


def waves(bins):
    angle = PHASE * np.mod(np.arange(QUARTER)[:, None] * (bins + FIRST_BIN)[None, :], SAMPLES)
    return np.cos(angle), np.sin(angle)


def even_table(bins):
    cos, sin = waves(bins)
    return padded(np.concatenate([cos, -sin], axis=1))


def odd_table(bins):
    cos, sin = waves(bins)
    turn = np.where((bins + FIRST_BIN) % 4 == 1, 1.0, -1.0)[None, :]
    first = np.concatenate([cos, -sin], axis=1)
    second = np.concatenate([-turn * sin, -turn * cos], axis=1)
    return np.concatenate([padded(first), padded(second)], axis=0)


def lag_table():
    shifts = np.arange(LAGS) - LAGS // 2
    angle = PHASE * np.mod((BINS_AT + FIRST_BIN)[:, None] * shifts[None, :], SAMPLES)
    table = np.zeros((2 * BINS, LAGS_PAD))
    table[:BINS, :LAGS] = np.cos(angle)
    table[BINS:, :LAGS] = -np.sin(angle)
    return bf16(table / 128.0)


def smoother():
    index = np.arange(BINS)
    inside = (np.abs(index[:, None] - index[None, :]) <= SMOOTH).astype(np.float32)
    mean = inside / np.sum(inside, axis=0, keepdims=True, dtype=np.float32)
    return mean[BINS_AT][:, BINS_AT]


def whiten_kernel(
    record, weight, taper, band, smooth, even0, even2, odd, plain, weighted, parts, table0, table2, table1, done
):
    fetches = [
        pltpu.make_async_copy(source, target, done.at[n])
        for n, (source, target) in enumerate(((even0, table0), (even2, table2), (odd, table1)))
    ]
    for fetch in fetches:
        fetch.start()
    for pair in range(4):
        value = jnp.concatenate([record[2 * pair], record[2 * pair + 1]], axis=0)
        value = value.astype(jnp.float32)
        mean = jnp.sum(value, axis=1, keepdims=True) * (1.0 / SAMPLES)
        centered = ((value - mean) * taper[...]).astype(jnp.bfloat16).astype(jnp.float32)
        quarter = [centered[:, QUARTER * q : QUARTER * (q + 1)] for q in range(4)]
        sum02, dif02 = quarter[0] + quarter[2], quarter[0] - quarter[2]
        sum13, dif13 = quarter[1] + quarter[3], quarter[1] - quarter[3]
        rows = slice(pair * 16, pair * 16 + 16)
        for n, part in enumerate((sum02 + sum13, sum02 - sum13, dif02, dif13)):
            parts[n, rows, :QUARTER] = part.astype(jnp.bfloat16)
            parts[n, rows, QUARTER:] = jnp.zeros((16, QUARTER_PAD - QUARTER), jnp.bfloat16)

    def product(n, table):
        return jnp.dot(parts[n], table, preferred_element_type=jnp.float32)

    fetches[0].wait()
    spec0 = product(0, table0[...])
    fetches[1].wait()
    spec2 = product(1, table2[...])
    fetches[2].wait()
    spec1 = product(2, table1[:QUARTER_PAD]) + product(3, table1[QUARTER_PAD:])
    scale = 1.0 / math.sqrt(SAMPLES)
    real_part = jnp.concatenate([spec0[:, :128], spec2[:, :128], spec1[:, :256]], axis=1) * scale
    imag_part = jnp.concatenate([spec0[:, 128:], spec2[:, 128:], spec1[:, 256:]], axis=1) * scale
    power = real_part * real_part + imag_part * imag_part
    smoothed = jnp.dot(
        power,
        smooth[...],
        precision=lax.Precision.HIGHEST,
        preferred_element_type=jnp.float32,
    )
    gain = band[...] / jnp.sqrt(smoothed + 1e-05)
    whitened = jnp.concatenate([real_part * gain, imag_part * gain], axis=1)
    for w in range(8):
        rows = whitened[8 * w : 8 * w + 8]
        plain[w] = rows.astype(jnp.bfloat16)
        weighted[w] = (rows * weight[w]).astype(jnp.bfloat16)


def full(shape):
    return pl.BlockSpec(shape, lambda j: (0,) * len(shape))


def whiten(record, weights):
    windows, channels, length = record.shape
    anywhere = pl.BlockSpec(memory_space=pltpu.HBM)
    out = jax.ShapeDtypeStruct((windows, channels, 2 * BINS), jnp.bfloat16)
    return pl.pallas_call(
        whiten_kernel,
        out_shape=(out, out),
        grid=(1,),
        in_specs=[
            full(record.shape),
            pl.BlockSpec(memory_space=pltpu.SMEM),
            full((1, SAMPLES)),
            full((1, BINS)),
            full((BINS, BINS)),
            anywhere,
            anywhere,
            anywhere,
        ],
        out_specs=(full(out.shape), full(out.shape)),
        scratch_shapes=[
            pltpu.VMEM((4, windows * channels, QUARTER_PAD), jnp.bfloat16),
            pltpu.VMEM((QUARTER_PAD, 256), jnp.bfloat16),
            pltpu.VMEM((QUARTER_PAD, 256), jnp.bfloat16),
            pltpu.VMEM((2 * QUARTER_PAD, 512), jnp.bfloat16),
            pltpu.SemaphoreType.DMA((3,)),
        ],
        compiler_params=pltpu.CompilerParams(vmem_limit_bytes=62 * 1024 * 1024),
        cost_estimate=pl.CostEstimate(
            flops=10**9, bytes_accessed=12 * 2**20, transcendentals=32768
        ),
    )(
        record,
        weights,
        time_taper()[None, :],
        band_taper()[BINS_AT][None, :],
        smoother(),
        even_table(BINS_AT[:128]),
        even_table(BINS_AT[128:256]),
        odd_table(BINS_AT[256:]),
    )


def device_at(x, y, z, core):
    return ((z % 4) * 8 + (z // 4) * 4 + x) * 8 + y * 2 + core


def shift(value, dx=0, dy=0, dz=0, dcore=0):
    pairs = [
        (
            device_at(x, y, z, core),
            device_at((x + dx) % 4, (y + dy) % 4, (z + dz) % 8, (core + dcore) % 2),
        )
        for x in range(4)
        for y in range(4)
        for z in range(8)
        for core in range(2)
    ]
    return lax.ppermute(value, AXES, pairs)


def own_only(value, k):
    return lax.ppermute(value, "win", [(i, (i + k) % 4) for i in range(4)])


def together(*values):
    return lax.optimization_barrier(values)


def first_step(plain, weighted):
    weighted, across = together(weighted, shift(plain, dx=2))
    return together(
        shift(weighted, dy=1),
        shift(weighted, dy=3),
        shift(weighted, dy=2),
        across,
        shift(plain, dz=2),
        shift(plain, dz=-3),
    )


def second_step(plain, weighted, arrived, y, z_low):
    left, right, opposite, across, behind, ahead = arrived
    near = jnp.stack([plain, ahead, behind])
    held = [weighted, left, opposite, right]

    def for_offset(k):
        at = (y - z_low - k) % 4
        low = jnp.where(at == 0, held[0], held[1])
        high = jnp.where(at == 2, held[2], held[3])
        return jnp.where(at < 2, low, high)

    return together(
        for_offset(0),
        own_only(for_offset(1), 1),
        own_only(for_offset(2), 2),
        own_only(for_offset(3), 3),
        shift(near, dx=-1),
        shift(near, dx=1),
        near,
        across,
    )


def third_step(arrived):
    *rows, right, left, near, across = arrived
    mine = jnp.stack(rows)
    across_near, other, down, up, *rest = together(
        shift(near[1:], dx=2),
        shift(mine, dcore=1),
        shift(near[:2], dz=-1),
        shift(near, dz=1),
        mine,
        near,
        left,
        right,
        across,
    )
    mine, near, left, right, across = rest
    return near, up, down, left, right, across, across_near, mine, other


def fourth_step(up, down, across, across_near):
    far = jnp.concatenate([up, down])
    down_out, up_out, right, left = together(
        shift(jnp.stack([across, across_near[0]]), dz=-1),
        shift(jnp.concatenate([across[None], across_near]), dz=1),
        shift(far, dx=-1),
        shift(far, dx=1),
    )
    return left, right, up_out, down_out


NEAR = (0, 3, -2)
FAR = (-1, 2, -3, 1, 4)
XS, HIGH, GROUP, ROWS, CORE = 0, 4, 12, 20, 24


def load_rows(place, mine, other, z_re, z_im, z_sum):
    core = place[CORE]
    for k in range(4):
        group = place[ROWS + k]
        for ref, at in ((mine, core), (other, 1 - core)):
            for w in range(8):
                value = ref[k, w].astype(jnp.float32)
                re, im = value[:, :BINS], value[:, BINS:]
                for tile in range(4):
                    lanes = slice(tile * 128, tile * 128 + 128)
                    z_re[group * 8 + w, at, tile] = re[:, lanes]
                    z_im[group * 8 + w, at, tile] = im[:, lanes]
                    z_sum[group * 8 + w, at, tile] = re[:, lanes] + im[:, lanes]


def add_cross(tile, block, high, group, rows, total):
    z_re, z_im, z_sum = rows
    lane = pl.ds(pl.multiple_of(tile * 128, 128), 128)
    lane_im = pl.ds(pl.multiple_of(tile * 128 + BINS, 128), 128)
    for core, base in ((0, 0), (0, 4), (1, 0), (1, 4)):
        sums = [None] * 12
        for w in range(8):
            yr = block[w, :, lane].astype(jnp.float32)
            yi = block[w, :, lane_im].astype(jnp.float32)
            dif = yr - yi
            window = group * 8 + w
            for i in range(4):
                row = pl.ds(base + i, 8, stride=0)
                terms = (
                    z_re[window, core, tile, row, :] * yr,
                    z_im[window, core, tile, row, :] * yi,
                    z_sum[window, core, tile, row, :] * dif,
                )
                for m, term in enumerate(terms):
                    at = i * 3 + m
                    sums[at] = term if w == 0 else sums[at] + term
        for i in range(4):
            p, q, r = sums[i * 3 : i * 3 + 3]
            total[high, core * 8 + base + i, :, lane] += p + q
            total[high, core * 8 + base + i, :, lane_im] += r - p + q


def add_blocks(blocks, place, first, rows, total):
    def tile_step(tile, carry):
        for n, block in enumerate(blocks, first):
            add_cross(tile, block, place[HIGH + n], place[GROUP + n], rows, total)
        return carry

    lax.fori_loop(0, 4, tile_step, 0)


def settle(source, target):
    for i in range(16):
        rows = jnp.concatenate([source[0, i], source[1, i]], axis=0)
        target[pl.ds(i * 16, 16), :] = rows.astype(jnp.bfloat16)


def parts_of(*refs):
    return [ref.at[n] for ref in refs for n in range(ref.shape[0])]


def near_kernel(
    place, near, up, down, left, right, across, across_near, mine, other, own, total, z_re, z_im, z_sum, sums
):
    rows = (z_re, z_im, z_sum)
    load_rows(place, mine, other, *rows)
    sums[...] = jnp.zeros_like(sums)
    total[...] = jnp.zeros_like(total)
    add_blocks(parts_of(near, up, down), place, 0, rows, sums)
    settle(sums, own)
    sides = (parts_of(left), parts_of(right), [across, *parts_of(across_near)])
    for n, blocks in enumerate(sides):
        add_blocks(blocks, place, 0, rows, total.at[n])


TOTAL = (2, 16, 8, 2 * BINS)
OWN = (256, 2 * BINS)
ROW_SCRATCH = [pltpu.VMEM((32, 2, 4, 8, 128), jnp.float32)] * 3


def whole(shape):
    return pl.BlockSpec(shape, lambda j, place: (0,) * len(shape))


def near_totals(place, *blocks):
    return pl.pallas_call(
        near_kernel,
        out_shape=(
            jax.ShapeDtypeStruct(OWN, jnp.bfloat16),
            jax.ShapeDtypeStruct((3, *TOTAL), jnp.float32),
        ),
        grid_spec=pltpu.PrefetchScalarGridSpec(
            num_scalar_prefetch=1,
            grid=(1,),
            in_specs=[whole(block.shape) for block in blocks],
            out_specs=(whole(OWN), whole((3, *TOTAL))),
            scratch_shapes=[*ROW_SCRATCH, pltpu.VMEM(TOTAL, jnp.float32)],
        ),
        compiler_params=pltpu.CompilerParams(vmem_limit_bytes=28 * 1024 * 1024),
        cost_estimate=pl.CostEstimate(
            flops=12 * 10**9, bytes_accessed=8 * 2**20, transcendentals=0
        ),
    )(place, *blocks)


def far_kernel(
    place, left, right, up, down, own, before, mine, other, source, out, z_re, z_im, z_sum, total, now, later, table, ready
):
    step = pl.program_id(0)
    fetch = pltpu.make_async_copy(source, table, ready)
    rows = (z_re, z_im, z_sum)

    @pl.when(step == 0)
    def _():
        fetch.start()
        load_rows(place, mine, other, *rows)
        now[...] = own[...]

    chunks = (parts_of(left), parts_of(right), parts_of(up, down))
    for n, blocks in enumerate(chunks):

        @pl.when(step == n)
        def _():
            total[...] = before[0]
            add_blocks(blocks, place, 3, rows, total)
            settle(total, later)

    @pl.when(step == 0)
    def _():
        fetch.wait()

    for tile in range(8):
        start = tile * 512
        keep = min(512, LAGS - start)
        value = jnp.dot(
            now[...], table[:, start : start + 512], preferred_element_type=jnp.float32
        )
        value = value.reshape(16, 2, 1, 8, 512).astype(jnp.bfloat16)
        out[:, :, :, :, start : start + keep] = value[..., :keep]

    @pl.when(step < 3)
    def _():
        now[...] = later[...]


def correlations(place, left, right, up, down, own, before, mine, other):
    return pl.pallas_call(
        far_kernel,
        out_shape=jax.ShapeDtypeStruct((16, 2, 4, 8, LAGS), jnp.bfloat16),
        grid_spec=pltpu.PrefetchScalarGridSpec(
            num_scalar_prefetch=1,
            grid=(4,),
            in_specs=[
                *[whole(block.shape) for block in (left, right, up, down, own)],
                pl.BlockSpec((1, *TOTAL), lambda j, place: (jnp.minimum(j, 2), 0, 0, 0, 0)),
                *[whole(block.shape) for block in (mine, other)],
                pl.BlockSpec(memory_space=pl.ANY),
            ],
            out_specs=pl.BlockSpec((16, 2, 1, 8, LAGS), lambda j, place: (0, 0, place[j], 0, 0)),
            scratch_shapes=[
                *ROW_SCRATCH,
                pltpu.VMEM(TOTAL, jnp.float32),
                pltpu.VMEM((256, 2 * BINS), jnp.bfloat16),
                pltpu.VMEM((256, 2 * BINS), jnp.bfloat16),
                pltpu.VMEM((2 * BINS, LAGS_PAD), jnp.bfloat16),
                pltpu.SemaphoreType.DMA(()),
            ],
        ),
        compiler_params=pltpu.CompilerParams(vmem_limit_bytes=36 * 1024 * 1024),
        cost_estimate=pl.CostEstimate(
            flops=2 * 1024 * 1024 * LAGS, bytes_accessed=24 * 2**20, transcendentals=0
        ),
    )(place, left, right, up, down, own, before, mine, other, lag_table())


def shards(record, window_weight):
    plain, weighted = whiten(record, window_weight)
    z_low = lax.axis_index("win")
    row = lax.axis_index("row")
    col = lax.axis_index("col")
    x, z = row % 4, (row // 4) * 4 + z_low
    where = (z + jnp.array(NEAR + FAR)) % 8
    place = jnp.concatenate(
        [
            (x + jnp.array([0, -1, 1, 2])) % 4,
            where // 4,
            where % 4,
            (z_low - jnp.arange(4)) % 4,
            jnp.stack([col % 2]),
        ]
    ).astype(jnp.int32)
    arrived = first_step(plain, weighted)
    arrived = second_step(plain, weighted, arrived, col // 2, z_low)
    near, up, down, left, right, across, across_near, mine, other = third_step(arrived)
    rest = fourth_step(up, down, across, across_near)
    own, before = near_totals(
        place, near, up, down, left, right, across, across_near, mine, other
    )
    corr = correlations(place, *rest, own, before, mine, other)
    return corr.reshape(1, 1, 16, 8, 8, LAGS)


def solution(mesh):
    placed = (P("win", ("row", "col"), None), P("win"))
    return jax.shard_map(
        shards,
        mesh=mesh,
        in_specs=placed,
        out_specs=P("row", "win", None, None, "col", None),
        check_vma=False,
    )
```

```python
import math

import jax
import jax.numpy as jnp
import ml_dtypes
import numpy as np
from jax import lax
from jax.experimental import pallas as pl
from jax.experimental.pallas import tpu as pltpu
from jax.sharding import PartitionSpec as P

SAMPLES = 12000
QUARTER = 3000
QUARTER_PAD = 3072
BINS = 512
LAGS = 4000
LAGS_PAD = 4096
FIRST_BIN = 60
SMOOTH = 64
AXES = ("win", "row", "col")
BINS_AT = np.concatenate([np.arange(0, 512, 4), np.arange(2, 512, 4), np.arange(1, 512, 2)])
PHASE = 2.0 * np.pi / SAMPLES


def bf16(values):
    return values.astype(np.float32).astype(ml_dtypes.bfloat16)


def time_taper():
    index = np.arange(SAMPLES)
    edge = np.minimum(index, SAMPLES - 1 - index).astype(np.float64)
    ramp = max(SAMPLES // 20, 1)
    return np.where(edge < ramp, 0.5 - 0.5 * np.cos(np.pi * (edge + 0.5) / ramp), 1.0).astype(
        np.float32
    )


def band_taper():
    index = np.arange(BINS)
    edge = np.minimum(index, BINS - 1 - index).astype(np.float64)
    ramp = max(BINS // 16, 1)
    return np.where(edge < ramp, 0.5 - 0.5 * np.cos(np.pi * (edge + 1.0) / (ramp + 1.0)), 1.0).astype(
        np.float32
    )


def padded(table):
    return bf16(np.pad(table, ((0, QUARTER_PAD - QUARTER), (0, 0))))


def waves(bins):
    angle = PHASE * np.mod(np.arange(QUARTER)[:, None] * (bins + FIRST_BIN)[None, :], SAMPLES)
    return np.cos(angle), np.sin(angle)


def even_table(bins):
    cos, sin = waves(bins)
    return padded(np.concatenate([cos, -sin], axis=1))


def odd_table(bins):
    cos, sin = waves(bins)
    turn = np.where((bins + FIRST_BIN) % 4 == 1, 1.0, -1.0)[None, :]
    first = np.concatenate([cos, -sin], axis=1)
    second = np.concatenate([-turn * sin, -turn * cos], axis=1)
    return np.concatenate([padded(first), padded(second)], axis=0)


def lag_table():
    shifts = np.arange(LAGS) - LAGS // 2
    angle = PHASE * np.mod((BINS_AT + FIRST_BIN)[:, None] * shifts[None, :], SAMPLES)
    table = np.zeros((2 * BINS, LAGS_PAD))
    table[:BINS, :LAGS] = np.cos(angle)
    table[BINS:, :LAGS] = -np.sin(angle)
    return bf16(table / 128.0)


def smoother():
    index = np.arange(BINS)
    inside = (np.abs(index[:, None] - index[None, :]) <= SMOOTH).astype(np.float32)
    mean = inside / np.sum(inside, axis=0, keepdims=True, dtype=np.float32)
    return mean[BINS_AT][:, BINS_AT]


def whiten_kernel(
    record, weight, taper, band, smooth, even0, even2, odd, plain, weighted, parts, table0, table2, table1, done
):
    fetches = [
        pltpu.make_async_copy(source, target, done.at[n])
        for n, (source, target) in enumerate(((even0, table0), (even2, table2), (odd, table1)))
    ]
    for fetch in fetches:
        fetch.start()
    for pair in range(4):
        value = jnp.concatenate([record[2 * pair], record[2 * pair + 1]], axis=0)
        value = value.astype(jnp.float32)
        mean = jnp.sum(value, axis=1, keepdims=True) * (1.0 / SAMPLES)
        centered = ((value - mean) * taper[...]).astype(jnp.bfloat16).astype(jnp.float32)
        quarter = [centered[:, QUARTER * q : QUARTER * (q + 1)] for q in range(4)]
        sum02, dif02 = quarter[0] + quarter[2], quarter[0] - quarter[2]
        sum13, dif13 = quarter[1] + quarter[3], quarter[1] - quarter[3]
        rows = slice(pair * 16, pair * 16 + 16)
        for n, part in enumerate((sum02 + sum13, sum02 - sum13, dif02, dif13)):
            parts[n, rows, :QUARTER] = part.astype(jnp.bfloat16)
            parts[n, rows, QUARTER:] = jnp.zeros((16, QUARTER_PAD - QUARTER), jnp.bfloat16)

    def product(n, table):
        return jnp.dot(parts[n], table, preferred_element_type=jnp.float32)

    fetches[0].wait()
    spec0 = product(0, table0[...])
    fetches[1].wait()
    spec2 = product(1, table2[...])
    fetches[2].wait()
    spec1 = product(2, table1[:QUARTER_PAD]) + product(3, table1[QUARTER_PAD:])
    scale = 1.0 / math.sqrt(SAMPLES)
    real_part = jnp.concatenate([spec0[:, :128], spec2[:, :128], spec1[:, :256]], axis=1) * scale
    imag_part = jnp.concatenate([spec0[:, 128:], spec2[:, 128:], spec1[:, 256:]], axis=1) * scale
    power = real_part * real_part + imag_part * imag_part
    smoothed = jnp.dot(
        power,
        smooth[...],
        precision=lax.Precision.HIGHEST,
        preferred_element_type=jnp.float32,
    )
    gain = band[...] / jnp.sqrt(smoothed + 1e-05)
    whitened = jnp.concatenate([real_part * gain, imag_part * gain], axis=1)
    for w in range(8):
        rows = whitened[8 * w : 8 * w + 8]
        plain[w] = rows.astype(jnp.bfloat16)
        weighted[w] = (rows * weight[w]).astype(jnp.bfloat16)


def full(shape):
    return pl.BlockSpec(shape, lambda j: (0,) * len(shape))


def whiten(record, weights):
    windows, channels, length = record.shape
    anywhere = pl.BlockSpec(memory_space=pltpu.HBM)
    out = jax.ShapeDtypeStruct((windows, channels, 2 * BINS), jnp.bfloat16)
    return pl.pallas_call(
        whiten_kernel,
        out_shape=(out, out),
        grid=(1,),
        in_specs=[
            full(record.shape),
            pl.BlockSpec(memory_space=pltpu.SMEM),
            full((1, SAMPLES)),
            full((1, BINS)),
            full((BINS, BINS)),
            anywhere,
            anywhere,
            anywhere,
        ],
        out_specs=(full(out.shape), full(out.shape)),
        scratch_shapes=[
            pltpu.VMEM((4, windows * channels, QUARTER_PAD), jnp.bfloat16),
            pltpu.VMEM((QUARTER_PAD, 256), jnp.bfloat16),
            pltpu.VMEM((QUARTER_PAD, 256), jnp.bfloat16),
            pltpu.VMEM((2 * QUARTER_PAD, 512), jnp.bfloat16),
            pltpu.SemaphoreType.DMA((3,)),
        ],
        compiler_params=pltpu.CompilerParams(vmem_limit_bytes=62 * 1024 * 1024),
        cost_estimate=pl.CostEstimate(
            flops=10**9, bytes_accessed=12 * 2**20, transcendentals=32768
        ),
    )(
        record,
        weights,
        time_taper()[None, :],
        band_taper()[BINS_AT][None, :],
        smoother(),
        even_table(BINS_AT[:128]),
        even_table(BINS_AT[128:256]),
        odd_table(BINS_AT[256:]),
    )


def device_at(x, y, z, core):
    return ((z % 4) * 8 + (z // 4) * 4 + x) * 8 + y * 2 + core


def shift(value, dx=0, dy=0, dz=0, dcore=0):
    pairs = [
        (
            device_at(x, y, z, core),
            device_at((x + dx) % 4, (y + dy) % 4, (z + dz) % 8, (core + dcore) % 2),
        )
        for x in range(4)
        for y in range(4)
        for z in range(8)
        for core in range(2)
    ]
    return lax.ppermute(value, AXES, pairs)


def own_only(value, k):
    return lax.ppermute(value, "win", [(i, (i + k) % 4) for i in range(4)])


def together(*values):
    return lax.optimization_barrier(values)


def first_step(plain, weighted):
    weighted, across = together(weighted, shift(plain, dx=2))
    return together(
        shift(weighted, dy=1),
        shift(weighted, dy=3),
        shift(weighted, dy=2),
        across,
        shift(plain, dz=2),
        shift(plain, dz=-3),
    )


def second_step(plain, weighted, arrived, y, z_low):
    left, right, opposite, across, behind, ahead = arrived
    near = jnp.stack([plain, ahead, behind])
    held = [weighted, left, opposite, right]

    def for_offset(k):
        at = (y - z_low - k) % 4
        low = jnp.where(at == 0, held[0], held[1])
        high = jnp.where(at == 2, held[2], held[3])
        return jnp.where(at < 2, low, high)

    return together(
        for_offset(0),
        own_only(for_offset(1), 1),
        own_only(for_offset(2), 2),
        own_only(for_offset(3), 3),
        shift(near, dx=-1),
        shift(near, dx=1),
        near,
        across,
    )


def third_step(arrived):
    *rows, right, left, near, across = arrived
    mine = jnp.stack(rows)
    across_near = shift(near[1:], dx=2)
    other = shift(mine, dcore=1)
    down = shift(near[:2], dz=-1)
    up = shift(near, dz=1)
    return near, up, down, left, right, across, across_near, mine, other


def fourth_step(up, down, left, right, across, across_near):
    far = jnp.concatenate([up, down[1:]])
    down_out, up_out, right_far, left_far = together(
        shift(jnp.stack([across, across_near[0], left[0], right[0]]), dz=-1),
        shift(jnp.concatenate([across[None], across_near]), dz=1),
        shift(far, dx=-1),
        shift(far, dx=1),
    )
    return left_far, right_far, up_out, down_out


NEAR = (0, 3, -2)
FAR = (-1, 2, -3, 1, 4)
XS, HIGH, GROUP, ROWS, CORE = 0, 4, 12, 20, 24


def load_rows(place, mine, other, z_re, z_im, z_sum):
    core = place[CORE]
    for k in range(4):
        group = place[ROWS + k]
        for ref, at in ((mine, core), (other, 1 - core)):
            for w in range(8):
                value = ref[k, w].astype(jnp.float32)
                re, im = value[:, :BINS], value[:, BINS:]
                for tile in range(4):
                    lanes = slice(tile * 128, tile * 128 + 128)
                    z_re[group * 8 + w, at, tile] = re[:, lanes]
                    z_im[group * 8 + w, at, tile] = im[:, lanes]
                    z_sum[group * 8 + w, at, tile] = re[:, lanes] + im[:, lanes]


def add_cross(tile, block, high, group, rows, total):
    z_re, z_im, z_sum = rows
    lane = pl.ds(pl.multiple_of(tile * 128, 128), 128)
    lane_im = pl.ds(pl.multiple_of(tile * 128 + BINS, 128), 128)
    for core, base in ((0, 0), (0, 4), (1, 0), (1, 4)):
        sums = [None] * 12
        for w in range(8):
            yr = block[w, :, lane].astype(jnp.float32)
            yi = block[w, :, lane_im].astype(jnp.float32)
            dif = yr - yi
            window = group * 8 + w
            for i in range(4):
                row = pl.ds(base + i, 8, stride=0)
                terms = (
                    z_re[window, core, tile, row, :] * yr,
                    z_im[window, core, tile, row, :] * yi,
                    z_sum[window, core, tile, row, :] * dif,
                )
                for m, term in enumerate(terms):
                    at = i * 3 + m
                    sums[at] = term if w == 0 else sums[at] + term
        for i in range(4):
            p, q, r = sums[i * 3 : i * 3 + 3]
            total[high, core * 8 + base + i, :, lane] += p + q
            total[high, core * 8 + base + i, :, lane_im] += r - p + q


def add_blocks(blocks, place, rows, total):
    def tile_step(tile, carry):
        for n, block in blocks:
            add_cross(tile, block, place[HIGH + n], place[GROUP + n], rows, total)
        return carry

    lax.fori_loop(0, 4, tile_step, 0)


def settle(source, target):
    for i in range(16):
        rows = jnp.concatenate([source[0, i], source[1, i]], axis=0)
        target[pl.ds(i * 16, 16), :] = rows.astype(jnp.bfloat16)


def parts_of(first, *refs):
    return list(enumerate([ref.at[n] for ref in refs for n in range(ref.shape[0])], first))


def lag_product(stack, table, out):
    for tile in range(8):
        start = tile * 512
        keep = min(512, LAGS - start)
        value = jnp.dot(
            stack[...], table[:, start : start + 512], preferred_element_type=jnp.float32
        )
        value = value.reshape(16, 2, 1, 8, 512).astype(jnp.bfloat16)
        out[:, :, :, :, start : start + keep] = value[..., :keep]


TOTAL = (2, 16, 8, 2 * BINS)
CORR = (16, 2, 4, 8, LAGS)
ROW_SCRATCH = [pltpu.VMEM((32, 2, 4, 8, 128), jnp.float32)] * 3
LAG_SCRATCH = [
    pltpu.VMEM((256, 2 * BINS), jnp.bfloat16),
    pltpu.VMEM((2 * BINS, LAGS_PAD), jnp.bfloat16),
    pltpu.SemaphoreType.DMA(()),
]


def whole(shape):
    return pl.BlockSpec(shape, lambda j, place: (0,) * len(shape))


def near_kernel(place, near, left, right, across, mine, other, kept, sides, z_re, z_im, z_sum):
    rows = (z_re, z_im, z_sum)
    load_rows(place, mine, other, *rows)
    kept[...] = jnp.zeros_like(kept)
    sides[...] = jnp.zeros_like(sides)
    add_blocks(parts_of(0, near), place, rows, kept.at[0])
    add_blocks([(0, across)], place, rows, kept.at[1])
    add_blocks(parts_of(0, left), place, rows, sides.at[0])
    add_blocks(parts_of(0, right), place, rows, sides.at[1])


def near_totals(place, *blocks):
    two = (2, *TOTAL)
    return pl.pallas_call(
        near_kernel,
        out_shape=(jax.ShapeDtypeStruct(two, jnp.float32),) * 2,
        grid_spec=pltpu.PrefetchScalarGridSpec(
            num_scalar_prefetch=1,
            grid=(1,),
            in_specs=[whole(block.shape) for block in blocks],
            out_specs=(whole(two), whole(two)),
            scratch_shapes=ROW_SCRATCH,
        ),
        compiler_params=pltpu.CompilerParams(vmem_limit_bytes=28 * 1024 * 1024),
        cost_estimate=pl.CostEstimate(
            flops=8 * 10**9, bytes_accessed=8 * 2**20, transcendentals=0
        ),
    )(place, *blocks)


def own_kernel(
    place, kept, up, down, across_near, mine, other, source, out, sum_across, z_re, z_im, z_sum, total, now, table, ready
):
    fetch = pltpu.make_async_copy(source, table, ready)
    fetch.start()
    rows = (z_re, z_im, z_sum)
    load_rows(place, mine, other, *rows)
    total[...] = kept[0]
    add_blocks(parts_of(3, up, down), place, rows, total)
    settle(total, now)
    sum_across[...] = kept[1]
    add_blocks(parts_of(1, across_near), place, rows, sum_across)
    fetch.wait()
    lag_product(now, table, out)


def own_correlations(place, *blocks):
    return pl.pallas_call(
        own_kernel,
        out_shape=(
            jax.ShapeDtypeStruct(CORR, jnp.bfloat16),
            jax.ShapeDtypeStruct(TOTAL, jnp.float32),
        ),
        grid_spec=pltpu.PrefetchScalarGridSpec(
            num_scalar_prefetch=1,
            grid=(1,),
            in_specs=[
                *[whole(block.shape) for block in blocks],
                pl.BlockSpec(memory_space=pl.ANY),
            ],
            out_specs=(
                pl.BlockSpec((16, 2, 1, 8, LAGS), lambda j, place: (0, 0, place[j], 0, 0)),
                whole(TOTAL),
            ),
            scratch_shapes=[*ROW_SCRATCH, pltpu.VMEM(TOTAL, jnp.float32), *LAG_SCRATCH],
        ),
        compiler_params=pltpu.CompilerParams(vmem_limit_bytes=36 * 1024 * 1024),
        cost_estimate=pl.CostEstimate(
            flops=10 * 10**9, bytes_accessed=16 * 2**20, transcendentals=0
        ),
    )(place, *blocks, lag_table())


def far_kernel(
    place, left, right, up, down, sides, sum_across, mine, other, begun, source, out, z_re, z_im, z_sum, total, now, table, ready
):
    step = pl.program_id(0)
    fetch = pltpu.make_async_copy(source, table, ready)
    rows = (z_re, z_im, z_sum)

    @pl.when(step == 0)
    def _():
        fetch.start()
        load_rows(place, mine, other, *rows)

    def of_side(side, extra):
        return [(3, side.at[0]), (4, side.at[1]), (5, side.at[2]), (7, side.at[3]), (6, extra)]

    chunks = (
        of_side(left, down.at[2]),
        of_side(right, down.at[3]),
        [*parts_of(3, up), (6, down.at[0]), (7, down.at[1])],
    )
    for n, blocks in enumerate(chunks):

        @pl.when(step == n)
        def _():
            total[...] = sides[0] if n < 2 else sum_across[...]
            add_blocks(blocks, place, rows, total)
            settle(total, now)

    @pl.when(step == 0)
    def _():
        fetch.wait()

    lag_product(now, table, out)


def correlations(place, begun, *blocks):
    left, right, up, down, sides, sum_across, mine, other = blocks
    anywhere = pl.BlockSpec(memory_space=pl.ANY)
    return pl.pallas_call(
        far_kernel,
        out_shape=jax.ShapeDtypeStruct(CORR, jnp.bfloat16),
        grid_spec=pltpu.PrefetchScalarGridSpec(
            num_scalar_prefetch=1,
            grid=(3,),
            in_specs=[
                *[whole(block.shape) for block in (left, right, up, down)],
                pl.BlockSpec((1, *TOTAL), lambda j, place: (jnp.minimum(j, 1), 0, 0, 0, 0)),
                *[whole(block.shape) for block in (sum_across, mine, other)],
                anywhere,
                anywhere,
            ],
            out_specs=pl.BlockSpec(
                (16, 2, 1, 8, LAGS), lambda j, place: (0, 0, place[j + 1], 0, 0)
            ),
            scratch_shapes=[*ROW_SCRATCH, pltpu.VMEM(TOTAL, jnp.float32), *LAG_SCRATCH],
        ),
        input_output_aliases={9: 0},
        compiler_params=pltpu.CompilerParams(vmem_limit_bytes=36 * 1024 * 1024),
        cost_estimate=pl.CostEstimate(
            flops=2 * 1024 * 1024 * LAGS, bytes_accessed=24 * 2**20, transcendentals=0
        ),
    )(place, *blocks, begun, lag_table())


def shards(record, window_weight):
    plain, weighted = whiten(record, window_weight)
    z_low = lax.axis_index("win")
    row = lax.axis_index("row")
    col = lax.axis_index("col")
    x, z = row % 4, (row // 4) * 4 + z_low
    where = (z + jnp.array(NEAR + FAR)) % 8
    place = jnp.concatenate(
        [
            (x + jnp.array([0, -1, 1, 2])) % 4,
            where // 4,
            where % 4,
            (z_low - jnp.arange(4)) % 4,
            jnp.stack([col % 2]),
        ]
    ).astype(jnp.int32)
    arrived = first_step(plain, weighted)
    arrived = second_step(plain, weighted, arrived, col // 2, z_low)
    near, up, down, left, right, across, across_near, mine, other = third_step(arrived)
    kept, sides = near_totals(place, near, left, right, across, mine, other)
    up, down, across_near, kept, sides = together(up, down, across_near, kept, sides)
    rest = fourth_step(up, down, left, right, across, across_near)
    corr, sum_across = own_correlations(place, kept, up, down, across_near, mine, other)
    corr = correlations(place, corr, *rest, sides, sum_across, mine, other)
    return corr.reshape(1, 1, 16, 8, 8, LAGS)


def solution(mesh):
    placed = (P("win", ("row", "col"), None), P("win"))
    return jax.shard_map(
        shards,
        mesh=mesh,
        in_specs=placed,
        out_specs=P("row", "win", None, None, "col", None),
        check_vma=False,
    )
```

```python
import math

import jax
import jax.numpy as jnp
import ml_dtypes
import numpy as np
from jax import lax
from jax.experimental import pallas as pl
from jax.experimental.pallas import tpu as pltpu
from jax.sharding import PartitionSpec as P

SAMPLES = 12000
QUARTER = 3000
QUARTER_PAD = 3072
BINS = 512
LAGS = 4000
LAGS_PAD = 4096
FIRST_BIN = 60
SMOOTH = 64
AXES = ("win", "row", "col")
BINS_AT = np.concatenate([np.arange(0, 512, 4), np.arange(2, 512, 4), np.arange(1, 512, 2)])
PHASE = 2.0 * np.pi / SAMPLES


def bf16(values):
    return values.astype(np.float32).astype(ml_dtypes.bfloat16)


def time_taper():
    index = np.arange(SAMPLES)
    edge = np.minimum(index, SAMPLES - 1 - index).astype(np.float64)
    ramp = max(SAMPLES // 20, 1)
    return np.where(edge < ramp, 0.5 - 0.5 * np.cos(np.pi * (edge + 0.5) / ramp), 1.0).astype(
        np.float32
    )


def band_taper():
    index = np.arange(BINS)
    edge = np.minimum(index, BINS - 1 - index).astype(np.float64)
    ramp = max(BINS // 16, 1)
    return np.where(edge < ramp, 0.5 - 0.5 * np.cos(np.pi * (edge + 1.0) / (ramp + 1.0)), 1.0).astype(
        np.float32
    )


def padded(table):
    return bf16(np.pad(table, ((0, QUARTER_PAD - QUARTER), (0, 0))))


def waves(bins):
    angle = PHASE * np.mod(np.arange(QUARTER)[:, None] * (bins + FIRST_BIN)[None, :], SAMPLES)
    return np.cos(angle), np.sin(angle)


def even_table(bins):
    cos, sin = waves(bins)
    return padded(np.concatenate([cos, -sin], axis=1))


def odd_table(bins):
    cos, sin = waves(bins)
    turn = np.where((bins + FIRST_BIN) % 4 == 1, 1.0, -1.0)[None, :]
    first = np.concatenate([cos, -sin], axis=1)
    second = np.concatenate([-turn * sin, -turn * cos], axis=1)
    return np.concatenate([padded(first), padded(second)], axis=0)


def lag_table():
    shifts = np.arange(LAGS) - LAGS // 2
    angle = PHASE * np.mod((BINS_AT + FIRST_BIN)[:, None] * shifts[None, :], SAMPLES)
    table = np.zeros((2 * BINS, LAGS_PAD))
    table[:BINS, :LAGS] = np.cos(angle)
    table[BINS:, :LAGS] = -np.sin(angle)
    return bf16(table / 128.0)


def smoother():
    index = np.arange(BINS)
    inside = (np.abs(index[:, None] - index[None, :]) <= SMOOTH).astype(np.float32)
    mean = inside / np.sum(inside, axis=0, keepdims=True, dtype=np.float32)
    return mean[BINS_AT][:, BINS_AT]


def whiten_kernel(
    record, weight, taper, band, smooth, even0, even2, odd, plain, weighted, parts, table0, table2, table1, done
):
    fetches = [
        pltpu.make_async_copy(source, target, done.at[n])
        for n, (source, target) in enumerate(((even0, table0), (even2, table2), (odd, table1)))
    ]
    for fetch in fetches:
        fetch.start()
    for pair in range(4):
        value = jnp.concatenate([record[2 * pair], record[2 * pair + 1]], axis=0)
        value = value.astype(jnp.float32)
        mean = jnp.sum(value, axis=1, keepdims=True) * (1.0 / SAMPLES)
        centered = ((value - mean) * taper[...]).astype(jnp.bfloat16).astype(jnp.float32)
        quarter = [centered[:, QUARTER * q : QUARTER * (q + 1)] for q in range(4)]
        sum02, dif02 = quarter[0] + quarter[2], quarter[0] - quarter[2]
        sum13, dif13 = quarter[1] + quarter[3], quarter[1] - quarter[3]
        rows = slice(pair * 16, pair * 16 + 16)
        for n, part in enumerate((sum02 + sum13, sum02 - sum13, dif02, dif13)):
            parts[n, rows, :QUARTER] = part.astype(jnp.bfloat16)
            parts[n, rows, QUARTER:] = jnp.zeros((16, QUARTER_PAD - QUARTER), jnp.bfloat16)

    def product(n, table):
        return jnp.dot(parts[n], table, preferred_element_type=jnp.float32)

    fetches[0].wait()
    spec0 = product(0, table0[...])
    fetches[1].wait()
    spec2 = product(1, table2[...])
    fetches[2].wait()
    spec1 = product(2, table1[:QUARTER_PAD]) + product(3, table1[QUARTER_PAD:])
    scale = 1.0 / math.sqrt(SAMPLES)
    real_part = jnp.concatenate([spec0[:, :128], spec2[:, :128], spec1[:, :256]], axis=1) * scale
    imag_part = jnp.concatenate([spec0[:, 128:], spec2[:, 128:], spec1[:, 256:]], axis=1) * scale
    power = real_part * real_part + imag_part * imag_part
    smoothed = jnp.dot(
        power,
        smooth[...],
        precision=lax.Precision.HIGHEST,
        preferred_element_type=jnp.float32,
    )
    gain = band[...] / jnp.sqrt(smoothed + 1e-05)
    whitened = jnp.concatenate([real_part * gain, imag_part * gain], axis=1)
    for w in range(8):
        rows = whitened[8 * w : 8 * w + 8]
        plain[w] = rows.astype(jnp.bfloat16)
        weighted[w] = (rows * weight[w]).astype(jnp.bfloat16)


def full(shape):
    return pl.BlockSpec(shape, lambda j: (0,) * len(shape))


def whiten(record, weights):
    windows, channels, length = record.shape
    anywhere = pl.BlockSpec(memory_space=pltpu.HBM)
    out = jax.ShapeDtypeStruct((windows, channels, 2 * BINS), jnp.bfloat16)
    return pl.pallas_call(
        whiten_kernel,
        out_shape=(out, out),
        grid=(1,),
        in_specs=[
            full(record.shape),
            pl.BlockSpec(memory_space=pltpu.SMEM),
            full((1, SAMPLES)),
            full((1, BINS)),
            full((BINS, BINS)),
            anywhere,
            anywhere,
            anywhere,
        ],
        out_specs=(full(out.shape), full(out.shape)),
        scratch_shapes=[
            pltpu.VMEM((4, windows * channels, QUARTER_PAD), jnp.bfloat16),
            pltpu.VMEM((QUARTER_PAD, 256), jnp.bfloat16),
            pltpu.VMEM((QUARTER_PAD, 256), jnp.bfloat16),
            pltpu.VMEM((2 * QUARTER_PAD, 512), jnp.bfloat16),
            pltpu.SemaphoreType.DMA((3,)),
        ],
        compiler_params=pltpu.CompilerParams(vmem_limit_bytes=62 * 1024 * 1024),
        cost_estimate=pl.CostEstimate(
            flops=10**9, bytes_accessed=12 * 2**20, transcendentals=32768
        ),
    )(
        record,
        weights,
        time_taper()[None, :],
        band_taper()[BINS_AT][None, :],
        smoother(),
        even_table(BINS_AT[:128]),
        even_table(BINS_AT[128:256]),
        odd_table(BINS_AT[256:]),
    )


def device_at(x, y, z, core):
    return ((z % 4) * 8 + (z // 4) * 4 + x) * 8 + y * 2 + core


def shift(value, dx=0, dy=0, dz=0, dcore=0):
    pairs = [
        (
            device_at(x, y, z, core),
            device_at((x + dx) % 4, (y + dy) % 4, (z + dz) % 8, (core + dcore) % 2),
        )
        for x in range(4)
        for y in range(4)
        for z in range(8)
        for core in range(2)
    ]
    return lax.ppermute(value, AXES, pairs)


def own_only(value, k):
    return lax.ppermute(value, "win", [(i, (i + k) % 4) for i in range(4)])


def together(*values):
    return lax.optimization_barrier(values)


def first_step(plain, weighted):
    return together(
        shift(weighted, dy=1),
        shift(weighted, dy=3),
        shift(weighted, dy=2),
        shift(plain, dx=2),
        shift(plain, dz=2),
        shift(plain, dz=-3),
    )


def second_step(plain, weighted, arrived, y, z_low):
    left, right, opposite, across, behind, ahead = arrived
    near = jnp.stack([plain, ahead, behind])
    held = [weighted, left, opposite, right]

    def for_offset(k):
        at = (y - z_low - k) % 4
        low = jnp.where(at == 0, held[0], held[1])
        high = jnp.where(at == 2, held[2], held[3])
        return jnp.where(at < 2, low, high)

    return together(
        for_offset(0),
        own_only(for_offset(1), 1),
        own_only(for_offset(2), 2),
        own_only(for_offset(3), 3),
        shift(near, dx=-1),
        shift(near, dx=1),
        near,
        across,
    )


def third_step(arrived):
    *rows, right, left, near, across = arrived
    mine = jnp.stack(rows)
    across_near = shift(near[1:], dx=2)
    other = shift(mine, dcore=1)
    down = shift(near[:2], dz=-1)
    up = shift(near, dz=1)
    return near, up, down, left, right, across, across_near, mine, other


def fourth_step(up, down, left, right, across, across_near):
    far = jnp.concatenate([up, down[1:]])
    down_out, up_out, right_far, left_far = together(
        shift(jnp.stack([across, across_near[0], left[0], right[0]]), dz=-1),
        shift(jnp.concatenate([across[None], across_near]), dz=1),
        shift(far, dx=-1),
        shift(far, dx=1),
    )
    return left_far, right_far, up_out, down_out


NEAR = (0, 3, -2)
FAR = (-1, 2, -3, 1, 4)
XS, HIGH, GROUP, ROWS, CORE = 0, 4, 12, 20, 24


def load_rows(place, mine, other, z_re, z_im, z_sum):
    core = place[CORE]
    for k in range(4):
        group = place[ROWS + k]
        for ref, at in ((mine, core), (other, 1 - core)):
            for w in range(8):
                value = ref[k, w].astype(jnp.float32)
                re, im = value[:, :BINS], value[:, BINS:]
                for tile in range(4):
                    lanes = slice(tile * 128, tile * 128 + 128)
                    z_re[group * 8 + w, at, tile] = re[:, lanes]
                    z_im[group * 8 + w, at, tile] = im[:, lanes]
                    z_sum[group * 8 + w, at, tile] = re[:, lanes] + im[:, lanes]


def add_cross(tile, block, high, group, rows, total):
    z_re, z_im, z_sum = rows
    lane = pl.ds(pl.multiple_of(tile * 128, 128), 128)
    lane_im = pl.ds(pl.multiple_of(tile * 128 + BINS, 128), 128)
    for core, base in ((0, 0), (0, 4), (1, 0), (1, 4)):
        sums = [None] * 12
        for w in range(8):
            yr = block[w, :, lane].astype(jnp.float32)
            yi = block[w, :, lane_im].astype(jnp.float32)
            dif = yr - yi
            window = group * 8 + w
            for i in range(4):
                row = pl.ds(base + i, 8, stride=0)
                terms = (
                    z_re[window, core, tile, row, :] * yr,
                    z_im[window, core, tile, row, :] * yi,
                    z_sum[window, core, tile, row, :] * dif,
                )
                for m, term in enumerate(terms):
                    at = i * 3 + m
                    sums[at] = term if w == 0 else sums[at] + term
        for i in range(4):
            p, q, r = sums[i * 3 : i * 3 + 3]
            total[high, core * 8 + base + i, :, lane] += p + q
            total[high, core * 8 + base + i, :, lane_im] += r - p + q


def add_blocks(blocks, place, rows, total):
    for n, block in blocks:
        def tile_step(tile, carry, n=n, block=block):
            add_cross(tile, block, place[HIGH + n], place[GROUP + n], rows, total)
            return carry

        lax.fori_loop(0, 4, tile_step, 0)


def settle(source, target):
    for i in range(16):
        rows = jnp.concatenate([source[0, i], source[1, i]], axis=0)
        target[pl.ds(i * 16, 16), :] = rows.astype(jnp.bfloat16)


def parts_of(first, *refs):
    return list(enumerate([ref.at[n] for ref in refs for n in range(ref.shape[0])], first))


def lag_product(stack, table, out):
    for tile in range(8):
        start = tile * 512
        keep = min(512, LAGS - start)
        value = jnp.dot(
            stack[...], table[:, start : start + 512], preferred_element_type=jnp.float32
        )
        value = value.reshape(16, 2, 1, 8, 512).astype(jnp.bfloat16)
        out[:, :, :, :, start : start + keep] = value[..., :keep]


TOTAL = (2, 16, 8, 2 * BINS)
CORR = (16, 2, 4, 8, LAGS)
ROW_SCRATCH = [pltpu.VMEM((32, 2, 4, 8, 128), jnp.float32)] * 3
LAG_SCRATCH = [
    pltpu.VMEM((256, 2 * BINS), jnp.bfloat16),
    pltpu.VMEM((2 * BINS, LAGS_PAD), jnp.bfloat16),
    pltpu.SemaphoreType.DMA(()),
]


def whole(shape):
    return pl.BlockSpec(shape, lambda j, place: (0,) * len(shape))


def near_kernel(place, near, left, right, across, mine, other, kept, sides, z_re, z_im, z_sum):
    rows = (z_re, z_im, z_sum)
    load_rows(place, mine, other, *rows)
    kept[...] = jnp.zeros_like(kept)
    sides[...] = jnp.zeros_like(sides)
    add_blocks(parts_of(0, near), place, rows, kept.at[0])
    add_blocks([(0, across)], place, rows, kept.at[1])
    add_blocks(parts_of(0, left), place, rows, sides.at[0])
    add_blocks(parts_of(0, right), place, rows, sides.at[1])


def near_totals(place, *blocks):
    two = (2, *TOTAL)
    return pl.pallas_call(
        near_kernel,
        out_shape=(jax.ShapeDtypeStruct(two, jnp.float32),) * 2,
        grid_spec=pltpu.PrefetchScalarGridSpec(
            num_scalar_prefetch=1,
            grid=(1,),
            in_specs=[whole(block.shape) for block in blocks],
            out_specs=(whole(two), whole(two)),
            scratch_shapes=ROW_SCRATCH,
        ),
        compiler_params=pltpu.CompilerParams(vmem_limit_bytes=28 * 1024 * 1024),
        cost_estimate=pl.CostEstimate(
            flops=8 * 10**9, bytes_accessed=8 * 2**20, transcendentals=0
        ),
    )(place, *blocks)


def own_kernel(
    place, kept, up, down, across_near, mine, other, source, out, sum_across, z_re, z_im, z_sum, total, now, table, ready
):
    fetch = pltpu.make_async_copy(source, table, ready)
    fetch.start()
    rows = (z_re, z_im, z_sum)
    load_rows(place, mine, other, *rows)
    total[...] = kept[0]
    add_blocks(parts_of(3, up, down), place, rows, total)
    settle(total, now)
    sum_across[...] = kept[1]
    add_blocks(parts_of(1, across_near), place, rows, sum_across)
    fetch.wait()
    lag_product(now, table, out)


def own_correlations(place, *blocks):
    return pl.pallas_call(
        own_kernel,
        out_shape=(
            jax.ShapeDtypeStruct(CORR, jnp.bfloat16),
            jax.ShapeDtypeStruct(TOTAL, jnp.float32),
        ),
        grid_spec=pltpu.PrefetchScalarGridSpec(
            num_scalar_prefetch=1,
            grid=(1,),
            in_specs=[
                *[whole(block.shape) for block in blocks],
                pl.BlockSpec(memory_space=pl.ANY),
            ],
            out_specs=(
                pl.BlockSpec((16, 2, 1, 8, LAGS), lambda j, place: (0, 0, place[j], 0, 0)),
                whole(TOTAL),
            ),
            scratch_shapes=[*ROW_SCRATCH, pltpu.VMEM(TOTAL, jnp.float32), *LAG_SCRATCH],
        ),
        compiler_params=pltpu.CompilerParams(vmem_limit_bytes=36 * 1024 * 1024),
        cost_estimate=pl.CostEstimate(
            flops=10 * 10**9, bytes_accessed=16 * 2**20, transcendentals=0
        ),
    )(place, *blocks, lag_table())


def far_kernel(
    place, left, right, up, down, sides, sum_across, mine, other, begun, source, out, z_re, z_im, z_sum, total, now, table, ready
):
    step = pl.program_id(0)
    fetch = pltpu.make_async_copy(source, table, ready)
    rows = (z_re, z_im, z_sum)

    @pl.when(step == 0)
    def _():
        fetch.start()
        load_rows(place, mine, other, *rows)

    def of_side(side, extra):
        return [(3, side.at[0]), (4, side.at[1]), (5, side.at[2]), (7, side.at[3]), (6, extra)]

    chunks = (
        of_side(left, down.at[2]),
        of_side(right, down.at[3]),
        [*parts_of(3, up), (6, down.at[0]), (7, down.at[1])],
    )
    for n, blocks in enumerate(chunks):

        @pl.when(step == n)
        def _():
            total[...] = sides[0] if n < 2 else sum_across[...]
            add_blocks(blocks, place, rows, total)
            settle(total, now)

    @pl.when(step == 0)
    def _():
        fetch.wait()

    lag_product(now, table, out)


def correlations(place, begun, *blocks):
    left, right, up, down, sides, sum_across, mine, other = blocks
    anywhere = pl.BlockSpec(memory_space=pl.ANY)
    return pl.pallas_call(
        far_kernel,
        out_shape=jax.ShapeDtypeStruct(CORR, jnp.bfloat16),
        grid_spec=pltpu.PrefetchScalarGridSpec(
            num_scalar_prefetch=1,
            grid=(3,),
            in_specs=[
                *[whole(block.shape) for block in (left, right, up, down)],
                pl.BlockSpec((1, *TOTAL), lambda j, place: (jnp.minimum(j, 1), 0, 0, 0, 0)),
                *[whole(block.shape) for block in (sum_across, mine, other)],
                anywhere,
                anywhere,
            ],
            out_specs=pl.BlockSpec(
                (16, 2, 1, 8, LAGS), lambda j, place: (0, 0, place[j + 1], 0, 0)
            ),
            scratch_shapes=[*ROW_SCRATCH, pltpu.VMEM(TOTAL, jnp.float32), *LAG_SCRATCH],
        ),
        input_output_aliases={9: 0},
        compiler_params=pltpu.CompilerParams(vmem_limit_bytes=36 * 1024 * 1024),
        cost_estimate=pl.CostEstimate(
            flops=2 * 1024 * 1024 * LAGS, bytes_accessed=24 * 2**20, transcendentals=0
        ),
    )(place, *blocks, begun, lag_table())


def shards(record, window_weight):
    plain, weighted = whiten(record, window_weight)
    z_low = lax.axis_index("win")
    row = lax.axis_index("row")
    col = lax.axis_index("col")
    x, z = row % 4, (row // 4) * 4 + z_low
    where = (z + jnp.array(NEAR + FAR)) % 8
    place = jnp.concatenate(
        [
            (x + jnp.array([0, -1, 1, 2])) % 4,
            where // 4,
            where % 4,
            (z_low - jnp.arange(4)) % 4,
            jnp.stack([col % 2]),
        ]
    ).astype(jnp.int32)
    arrived = first_step(plain, weighted)
    arrived = second_step(plain, weighted, arrived, col // 2, z_low)
    near, up, down, left, right, across, across_near, mine, other = third_step(arrived)
    kept, sides = near_totals(place, near, left, right, across, mine, other)
    up, down, across_near, kept, sides = together(up, down, across_near, kept, sides)
    rest = fourth_step(up, down, left, right, across, across_near)
    corr, sum_across = own_correlations(place, kept, up, down, across_near, mine, other)
    corr = correlations(place, corr, *rest, sides, sum_across, mine, other)
    return corr.reshape(1, 1, 16, 8, 8, LAGS)


def solution(mesh):
    placed = (P("win", ("row", "col"), None), P("win"))
    return jax.shard_map(
        shards,
        mesh=mesh,
        in_specs=placed,
        out_specs=P("row", "win", None, None, "col", None),
        check_vma=False,
    )
```
